32 devices in a mesh: worker: 8 (over y, x, core), fsdp: 4 (over z).
Axes of the slice: x: 2, y: 2, z: 4, core: 2. Of those that a mesh axis runs over, the one named last changes fastest.
Arguments:
- tokens: bfloat16 [2048, 8192], P('worker', 'fsdp'), may hold values from -6 to 6
- inner_weight: bfloat16 [8, 8192, 512], P('worker', 'fsdp'), may hold values from -0.0625 to 0.0625
- key_grad: bfloat16 [2048, 512], P(('worker', 'fsdp')), may hold values from -6 to 6
- anchor: float32 [8192, 512], P('fsdp'), may hold values from -0.0625 to 0.0625
- momentum: float32 [8192, 512], P('fsdp'), may hold values from -0.06 to 0.06
- stale_delta: bfloat16 [8, 8192, 512], P('worker', 'fsdp'), may hold values from -0.29882812 to 0.29882812
Outputs:
- keys: bfloat16 [2048, 512], P(('worker', 'fsdp'))
- input_grad: bfloat16 [2048, 8192], P('worker', 'fsdp')
- new_params: bfloat16 [8, 8192, 512], P('worker', 'fsdp')
- new_momentum: float32 [8192, 512], P(('fsdp', 'worker'))
- fresh_delta: bfloat16 [8, 8192, 512], P('worker', 'fsdp')
The draws below stay inside these ranges and needn't reach their ends.
All inputs are finite; a program needn't handle non-finite values.
Results may differ from the reference program's by a relative error of at most 0.001.
Values may be sent and summed in bfloat16 or wider, within the bound.
No kernel may reach another device: no remote copies, remote signals or barrier semaphores. Data moves between devices by JAX's collectives and lax.ppermute only.
A program may use at most 64 MiB of HBM per device.

```python
import jax
import jax.numpy as jnp
from jax import lax

D = 8192
TOK = 256
KW = 512
WORKERS = 8
TOKENS = 2048


def steps_of(stream_key, shape, shards, low, top_value):
    def one(axis_at, parts):
        heights = jax.random.uniform(jax.random.fold_in(jax.random.fold_in(stream_key, 6), axis_at), (parts,), jnp.float32, low / len(shards), top_value / len(shards))
        return jnp.repeat(jnp.exp(heights), shape[axis_at] // parts).reshape((-1,) + (1,) * (len(shape) - axis_at - 1))

    gain = one(*shards[0])
    for cut in shards[1:]:
        gain = gain * one(*cut)
    return gain


def noise(key, extent, width, bound, split=(), held_as=jnp.bfloat16):
    result = jax.random.normal(key, extent, jnp.float32) * width
    if len(split) > 0:
        result = steps_of(key, extent, split, -0.22, 0.18) * result
    return jnp.clip(result, min=-bound, max=bound).astype(held_as)


def setup_inputs(seed: int = 0) -> dict:
    key_list = jax.random.split(jax.random.key(seed), 7)
    tokens = noise(key_list[0], (TOKENS, D), 1.0, 6.0, ((0, 8), (1, 4)))
    inner_weight = noise(key_list[1], (WORKERS, D, KW), D ** -0.5, 0.0625, ((0, 8), (1, 4)))
    key_grad = noise(key_list[2], (TOKENS, KW), 1.0, 6.0, ((0, 32),))
    anchor = noise(key_list[3], (D, KW), D ** -0.5, 0.0625, ((0, 4),), jnp.float32)
    momentum = noise(key_list[4], (D, KW), 0.01, 0.06, ((0, 4),), jnp.float32)
    stale_delta = noise(key_list[5], (WORKERS, D, KW), 0.05, 0.29882812, ((0, 8), (1, 4)))
    return dict(tokens=tokens, inner_weight=inner_weight, key_grad=key_grad, anchor=anchor, momentum=momentum, stale_delta=stale_delta)


inner_rate = 0.0005
outer_rate = 0.7
outer_momentum = 0.9


def reference(tokens, inner_weight, key_grad, anchor, momentum, stale_delta):
    summed = jnp.sum(stale_delta.astype(jnp.float32), axis=0)
    average = summed / WORKERS
    new_moment = outer_momentum * momentum + average
    common_term = average + outer_momentum * new_moment
    token_blocks = tokens.reshape(WORKERS, TOK, D)
    grad_blocks = key_grad.reshape(WORKERS, TOK, KW)

    def one_worker(operands):
        inputs, weights, upstream, stale_value = operands
        key_out = jnp.dot(inputs, weights, preferred_element_type=jnp.float32).astype(jnp.bfloat16)
        grad_weight = jnp.dot(inputs.T, upstream, preferred_element_type=jnp.float32)
        grad_input = jnp.dot(upstream, weights.T, preferred_element_type=jnp.float32).astype(jnp.bfloat16)
        fresh_term = anchor - (weights.astype(jnp.float32) - inner_rate * grad_weight)
        updated = anchor - outer_rate * (common_term + (fresh_term - stale_value.astype(jnp.float32)) / WORKERS)
        return key_out, grad_input, updated.astype(jnp.bfloat16), fresh_term.astype(jnp.bfloat16)

    key_all, grad_all, updated_all, fresh_all = lax.map(one_worker, (token_blocks, inner_weight, grad_blocks, stale_delta))
    return key_all.reshape(TOKENS, KW), grad_all.reshape(TOKENS, D), updated_all, new_moment, fresh_all
```

```python
import functools
import math

import jax
import jax.numpy as jnp
from jax import lax
from jax.experimental import pallas as pl
from jax.experimental.pallas import tpu as pltpu
from jax.sharding import PartitionSpec as P

inner_rate = 0.0005
outer_rate = 0.7
outer_momentum = 0.9

stale_bound = 0.29882812
floor = 2.0**-14
power = 250.0 / math.log2(1.0 + stale_bound / floor)


def encode(value, count):
    grown = jnp.log(jnp.abs(value) * (1.0 / (floor * count)) + 1.0)
    code = jnp.exp2(grown * (power / math.log(2.0)) - 125.0)
    return jnp.where(value < 0, -code, code).astype(jnp.bfloat16)


def decode(code, count):
    code = code.astype(jnp.float32)
    grown = jnp.exp2(jnp.log(jnp.abs(code)) * (1.0 / (power * math.log(2.0))) + 125.0 / power)
    value = (grown - 1.0) * (floor * count)
    return jnp.where(code < 0, -value, value)


def place(me):
    core, low, high = me % 2, (me // 2) % 2, me // 4
    return core, jnp.where(core == 0, low, high), jnp.where(core == 0, high, low)


def block(region, half, sub):
    return jnp.where(region == 0, 4 * sub + 2 * half, 4 * half + 2 * sub + 1)


def call(kernel, me, grid, ins, outs, scratch=(), aliases=None, flops=0, vmem=None):
    def spec(shape, index):
        if shape is None:
            return pl.BlockSpec(memory_space=pl.ANY)
        return pl.BlockSpec(shape, lambda i, me_ref: index(i, me_ref[0]))

    moved = sum(math.prod(s) * 4 * grid for _, s, _ in ins if s is not None)
    moved += sum(math.prod(s) * 4 * grid for _, _, s, _ in outs)
    return pl.pallas_call(
        kernel,
        grid_spec=pltpu.PrefetchScalarGridSpec(
            num_scalar_prefetch=1,
            grid=(grid,),
            in_specs=[spec(s, f) for _, s, f in ins],
            out_specs=[spec(s, f) for _, _, s, f in outs],
            scratch_shapes=scratch,
        ),
        out_shape=[jax.ShapeDtypeStruct(shape, dtype) for shape, dtype, _, _ in outs],
        input_output_aliases=aliases or {},
        cost_estimate=pl.CostEstimate(flops=flops, bytes_accessed=moved, transcendentals=0),
        compiler_params=pltpu.CompilerParams(vmem_limit_bytes=vmem or 32 * 2**20),
    )(me, *[a for a, _, _ in ins])


def copy_kernel(me_ref, value, out):
    out[...] = value[...]


def pair_kernel(me_ref, send_own, keep_own, send_other, keep_other, code, keep):
    f32 = jnp.float32
    code[...] = encode(send_own[...].astype(f32) + send_other[...].astype(f32), 2)
    keep[...] = keep_own[...].astype(f32) + keep_other[...].astype(f32)


def add_kernel(held, total, me_ref, value, received, out, code):
    summed = value[...] + decode(received[...], held)
    out[...] = summed
    code[...] = encode(summed, total)


def keys_kernel(parts, me_ref, tokens, weights, *rest):
    outs, total = rest[:parts], rest[parts]
    step = pl.program_id(0)
    product = jnp.dot(tokens[...], weights[...], preferred_element_type=jnp.float32)

    @pl.when(step == 0)
    def _():
        total[...] = product

    @pl.when(step > 0)
    def _():
        total[...] += product

    @pl.when(step == pl.num_programs(0) - 1)
    def _():
        rows = total.shape[0] // parts
        for d in range(parts):
            at = pl.multiple_of((me_ref[1] ^ d) * rows, rows)
            outs[d][...] = total[pl.ds(at, rows), :]


def fresh_kernel(parts, workers, filled, me_ref, tokens, weights, anchor, momentum, stale, *rest):
    grads, rest = rest[:parts], rest[parts:]
    if filled:
        rest = rest[3:]
    fresh_out, base_out, grad_out, portion = rest

    @pl.when(pl.program_id(0) == 0)
    def _():
        rows = grads[0].shape[0]
        for d in range(parts):
            at = pl.multiple_of((me_ref[1] ^ d) * rows, rows)
            portion[pl.ds(at, rows), :] = grads[d][...]

    grad_weight = lax.dot_general(
        tokens[...], portion[...], (((0,), (0,)), ((), ())), preferred_element_type=jnp.float32
    )
    grad_out[...] = lax.dot_general(
        portion[...], weights[...], (((1,), (1,)), ((), ())), preferred_element_type=jnp.float32
    ).astype(jnp.bfloat16)
    fresh = anchor[...] - (weights[...].astype(jnp.float32) - inner_rate * grad_weight)
    fresh_out[...] = fresh.astype(jnp.bfloat16)
    base_out[...] = anchor[...] - outer_rate * (
        outer_momentum * outer_momentum * momentum[...] + (fresh - stale[...].astype(jnp.float32)) / workers
    )


def final_kernel(subs, workers, kinds, filled, me_ref, base, *rest):
    pieces = rest[: len(kinds)]
    out = rest[-1]
    for at in range(len(kinds)):

        @pl.when(pl.program_id(0) // subs == at)
        def _(at=at):
            total = pieces[at][...]
            if kinds[at] != "own":
                total = decode(total, workers)
            out[...] = (base[...] - (outer_rate * (1.0 + outer_momentum) / workers) * total).astype(jnp.bfloat16)


chunk_subs = ((0,), (1,))


def fast(tokens, inner_weight, key_grad, anchor, momentum, stale_delta):
    workers, shards = lax.axis_size("worker"), lax.axis_size("fsdp")
    f32, bf16 = jnp.float32, jnp.bfloat16
    weights, stale = inner_weight[0], stale_delta[0]
    rows, columns = stale.shape
    size = rows // workers
    window = (size, columns)
    worker = lax.axis_index("worker")
    me = jnp.stack([worker, lax.axis_index("fsdp")]).astype(jnp.int32)

    def swap(value, flips):
        return lax.ppermute(value, "worker", [(i, i ^ flips[i % 2]) for i in range(workers)])

    beside, first, last = (1, 1), (2, 4), (4, 2)

    grads = [key_grad] + [
        lax.ppermute(key_grad, "fsdp", [(i, i ^ d) for i in range(shards)]) for d in range(1, shards)
    ]

    chunks = []
    for subs in chunk_subs:
        n, base = len(subs), subs[0]

        def other(i, me):
            core, _, _ = place(me)
            return block(1 - core, i // n, base + i % n), 0

        def mine(flip):
            def index(i, me):
                core, f, _ = place(me)
                return block(core, f ^ flip, base + i), 0

            return index

        def half(flip):
            def index(i, me):
                _, f, _ = place(me)
                return (f ^ flip) * n + i, 0

            return index

        straight = lambda i, me: (i, 0)
        (sent,) = call(
            copy_kernel, me, 2 * n, [(stale, window, other)], [((2 * n * size, columns), bf16, window, straight)]
        )
        received = swap(sent, beside)
        code, keep = call(
            pair_kernel,
            me,
            n,
            [
                (stale, window, mine(1)),
                (stale, window, mine(0)),
                (received, window, half(1)),
                (received, window, half(0)),
            ],
            [((n * size, columns), bf16, window, straight), ((n * size, columns), f32, window, straight)],
        )
        for held, total, flips in ((2, 4, first), (4, 8, last)):
            got = swap(code, flips)
            keep, code = call(
                functools.partial(add_kernel, held, total),
                me,
                n,
                [(keep, window, straight), (got, window, straight)],
                [((n * size, columns), f32, window, straight), ((n * size, columns), bf16, window, straight)],
            )
        near = swap(code, first)
        across = swap(code, beside)
        far = swap(near, beside)
        chunks.append((subs, keep, near, across, far))

    key_rows = tokens.shape[0] // shards
    partial = call(
        functools.partial(keys_kernel, shards),
        me,
        workers,
        [
            (tokens, (tokens.shape[0], size), lambda i, me: (0, i)),
            (weights, window, lambda i, me: (i, 0)),
        ],
        [((key_rows, columns), f32, (key_rows, columns), lambda i, me: (0, 0))] * shards,
        scratch=[pltpu.VMEM((tokens.shape[0], columns), f32)],
        flops=2 * tokens.shape[0] * rows * columns,
    )
    key_out = partial[0]
    for d in range(1, shards):
        key_out = key_out + lax.ppermute(partial[d], "fsdp", [(i, i ^ d) for i in range(shards)])
    key_out = key_out.astype(bf16)

    outs = None
    calls = 4
    per = workers // calls
    for at in range(calls):
        across_rows = lambda i, me, at=at: (at * per + i, 0)
        across_columns = lambda i, me, at=at: (0, at * per + i)
        ins = [
            (tokens, (tokens.shape[0], size), across_columns),
            (weights, window, across_rows),
            (anchor, window, across_rows),
            (momentum, window, across_rows),
            (stale, window, across_rows),
        ] + [(g, g.shape, lambda i, me: (0, 0)) for g in grads]
        aliases = {}
        if outs is not None:
            aliases = {1 + len(ins) + k: k for k in range(3)}
            ins += [(o, None, None) for o in outs]
        outs = call(
            functools.partial(fresh_kernel, shards, workers, outs is not None),
            me,
            per,
            ins,
            [
                ((rows, columns), bf16, window, across_rows),
                ((rows, columns), f32, window, across_rows),
                ((tokens.shape[0], rows), bf16, (tokens.shape[0], size), across_columns),
            ],
            scratch=[pltpu.VMEM((tokens.shape[0], columns), bf16)],
            aliases=aliases,
            flops=4 * tokens.shape[0] * rows * columns // calls,
        )
    fresh_out, base, grad_input = outs

    updated = None
    for at, (subs, keep, near, across, far) in enumerate(chunks):
        groups = [(("own", keep), ("across", across), ("near", near), ("far", far))]
        if at == len(chunks) - 1:
            groups = [(("own", keep), ("across", across)), (("near", near), ("far", far))]
        for group in groups:
            kinds = [k for k, _ in group]
            n = len(subs)

            def rows_of(i, me, kinds=kinds, n=n, subs=subs):
                core, f, l = place(me)
                spots = {"own": (core, f), "near": (core, 1 - f), "across": (1 - core, l), "far": (1 - core, 1 - l)}
                region, half = spots[kinds[0]]
                for k, kind in enumerate(kinds[1:], 1):
                    region = jnp.where(i // n == k, spots[kind][0], region)
                    half = jnp.where(i // n == k, spots[kind][1], half)
                return block(region, half, subs[0] + i % n), 0

            ins = [(base, window, rows_of)] + [
                (p, window, lambda i, me, k=k, n=n: (jnp.clip(i - k * n, 0, n - 1), 0))
                for k, (_, p) in enumerate(group)
            ]
            aliases = {}
            if updated is not None:
                aliases = {1 + len(ins): 0}
                ins.append((updated, None, None))
            (updated,) = call(
                functools.partial(final_kernel, n, workers, kinds, updated is not None),
                me,
                n * len(kinds),
                ins,
                [((rows, columns), bf16, window, rows_of)],
                aliases=aliases,
            )

    totals = jnp.concatenate([c[1] for c in chunks], 0).reshape(2, size, columns)
    _, _, l = place(worker)
    average = jnp.where(l == 0, totals[0], totals[1]) / workers
    new_moment = outer_momentum * lax.dynamic_slice_in_dim(momentum, worker * size, size, 0) + average
    return key_out, grad_input, updated[None], new_moment, fresh_out[None]


def plain(tokens, inner_weight, key_grad, anchor, momentum, stale_delta):
    weights = inner_weight[0]
    key_out = lax.psum_scatter(
        jnp.dot(tokens, weights, preferred_element_type=jnp.float32), "fsdp", scatter_dimension=0, tiled=True
    ).astype(jnp.bfloat16)
    portion = lax.all_gather(key_grad, "fsdp", axis=0, tiled=True)
    grad_weight = lax.dot_general(tokens, portion, (((0,), (0,)), ((), ())), preferred_element_type=jnp.float32)
    grad_input = lax.dot_general(portion, weights, (((1,), (1,)), ((), ())), preferred_element_type=jnp.float32)
    fresh_term = anchor - (weights.astype(jnp.float32) - inner_rate * grad_weight)
    stale_value = stale_delta[0].astype(jnp.float32)
    workers = lax.axis_size("worker")
    average = lax.psum(stale_value, "worker") / workers
    moment_full = outer_momentum * momentum + average
    common_term = average + outer_momentum * moment_full
    share_rows = anchor.shape[0] // workers
    new_moment = lax.dynamic_slice_in_dim(moment_full, lax.axis_index("worker") * share_rows, share_rows, 0)
    updated = anchor - outer_rate * (common_term + (fresh_term - stale_value) / workers)
    return (
        key_out,
        grad_input.astype(jnp.bfloat16),
        updated[None].astype(jnp.bfloat16),
        new_moment,
        fresh_term[None].astype(jnp.bfloat16),
    )


def local(*args):
    tokens, inner_weight = args[:2]
    workers, shards = lax.axis_size("worker"), lax.axis_size("fsdp")
    size = inner_weight.shape[1] // workers
    fits = workers == 2**3 and shards & (shards - 1) == 0
    fits = fits and size % 128 == 0 and tokens.shape[0] // shards % 16 == 0
    return (fast if fits else plain)(*args)


def solution(mesh):
    in_specs = (
        P("worker", "fsdp"),
        P("worker", "fsdp", None),
        P(("worker", "fsdp"), None),
        P("fsdp", None),
        P("fsdp", None),
        P("worker", "fsdp", None),
    )
    out_specs = (
        P(("worker", "fsdp"), None),
        P("worker", "fsdp"),
        P("worker", "fsdp", None),
        P(("fsdp", "worker"), None),
        P("worker", "fsdp", None),
    )
    return jax.shard_map(local, mesh=mesh, in_specs=in_specs, out_specs=out_specs, check_vma=False)
```

```python
import functools
import math

import jax
import jax.numpy as jnp
from jax import lax
from jax.experimental import pallas as pl
from jax.experimental.pallas import tpu as pltpu
from jax.sharding import PartitionSpec as P

inner_rate = 0.0005
outer_rate = 0.7
outer_momentum = 0.9

stale_bound = 0.29882812
floor = 2.0**-14
power = 250.0 / math.log2(1.0 + stale_bound / floor)


def encode(value, count):
    grown = jnp.log(jnp.abs(value) * (1.0 / (floor * count)) + 1.0)
    code = jnp.exp2(grown * (power / math.log(2.0)) - 125.0)
    return jnp.where(value < 0, -code, code).astype(jnp.bfloat16)


def decode(code, count):
    code = code.astype(jnp.float32)
    grown = jnp.exp2(jnp.log(jnp.abs(code)) * (1.0 / (power * math.log(2.0))) + 125.0 / power)
    value = (grown - 1.0) * (floor * count)
    return jnp.where(code < 0, -value, value)


pace = 3.3e9


def place(me):
    core, low, high = me % 2, (me // 2) % 2, me // 4
    return core, jnp.where(core == 0, low, high), jnp.where(core == 0, high, low)


def block(region, half, sub):
    return jnp.where(region == 0, 4 * sub + 2 * half, 4 * half + 2 * sub + 1)


SMEM, VMEM, HBM, ANY = pltpu.SMEM, pltpu.VMEM, pltpu.HBM, pl.ANY


def call(kernel, ins, outs, scratch=(), after=(), aliases=None, micros=1.0, vmem=12):
    late = len(after)

    def body(*refs):
        kernel(*refs[: len(ins)], *refs[len(ins) + late :])

    def placed(array, space):
        return pltpu.with_memory_space_constraint(array, space) if space in (HBM, VMEM) else array

    return pl.pallas_call(
        body,
        in_specs=[pl.BlockSpec(memory_space=s) for _, s in ins] + [pl.BlockSpec(memory_space=ANY)] * late,
        out_specs=[pl.BlockSpec(memory_space=s) for _, _, s in outs],
        out_shape=[s(shape, dtype) for shape, dtype, s in outs],
        scratch_shapes=scratch,
        input_output_aliases=aliases or {},
        cost_estimate=pl.CostEstimate(flops=int(micros * pace), bytes_accessed=0, transcendentals=0),
        compiler_params=pltpu.CompilerParams(vmem_limit_bytes=vmem * 2**20),
    )(*[placed(a, s) for a, s in ins], *after)


def rows(ref, at, size):
    return ref.at[pl.ds(pl.multiple_of(at * size, size), size), :]


def pair_kernel(size, sub, me_ref, stale, other, code, keep):
    core, first, _ = place(me_ref[0])

    def summed(half):
        at = block(core, half, sub)
        return rows(stale, at, size)[...].astype(jnp.float32) + rows(other, at, size)[...].astype(jnp.float32)

    code[...] = encode(summed(1 - first), 2)
    keep[...] = summed(first)


def add_kernel(held, total, value, received, out, code):
    summed = value[...] + decode(received[...], held)
    out[...] = summed
    code[...] = encode(summed, total)


def keys_kernel(me_ref, tokens, weights, sent, own, later, total):
    total[...] = jnp.dot(tokens[...], weights[...], preferred_element_type=jnp.float32)
    size = own.shape[0]
    shard = me_ref[1]
    sent[:size, :] = rows(total, shard ^ 1, size)[...]
    sent[size:, :] = rows(total, shard ^ 3, size)[...]
    own[...] = rows(total, shard, size)[...]
    later[...] = rows(total, shard ^ 2, size)[...]


def keys_add_kernel(received, own, later, own_out, later_out):
    size = own.shape[0]
    own_out[...] = own[...] + received[:size, :]
    later_out[...] = later[...] + received[size:, :]


def spots(me):
    core, first, last = place(me)
    return {
        "own": (core, first),
        "near": (core, 1 - first),
        "across": (1 - core, last),
        "far": (1 - core, 1 - last),
    }


def fresh_kernel(parts, workers, kinds, finish, me_ref, tokens, weights, anchor, momentum, stale, *rest):
    count = len(kinds)
    grads, rest = rest[:parts], rest[parts:]
    if finish:
        sums, partial, rest = rest[:count], rest[count : count + 2], rest[count + 4 :]
        fresh_out, grad_out, param_out, moment_out, key_out = rest[:5]
        param_buf, moment_buf, key_buf, rest = rest[5], rest[6], rest[7], rest[8:]
    else:
        fresh_out, grad_out, bases, rest = rest[0], rest[1], rest[2 : 2 + count], rest[2 + count :]
    portion, fresh_buf, grad_buf, sem = rest
    size = weights.shape[0] // workers
    known = spots(me_ref[0])
    spans = [pl.ds(pl.multiple_of(block(*known[kind], sub) * size, size), size) for kind, sub in kinds]
    departures = []

    def send(source, target):
        copy = pltpu.make_async_copy(source, target, sem.at[len(departures)])
        copy.start()
        departures.append(copy)

    if finish:
        key_buf[...] = (partial[0][...] + partial[1][...]).astype(jnp.bfloat16)
        send(key_buf, key_out)
        _, _, last = place(me_ref[0])
        average = jnp.where(last == 0, sums[0][...], sums[1][...]) / workers
        moment_buf[...] = outer_momentum * rows(momentum, me_ref[0], size)[...] + average
        send(moment_buf, moment_out)
    held = grads[0].shape[0]
    for d in range(parts):
        rows(portion, me_ref[1] ^ d, held)[...] = grads[d][...]
    for k, span in enumerate(spans):
        weight = weights[span, :]
        grad_weight = lax.dot_general(
            tokens[:, span], portion[...], (((0,), (0,)), ((), ())), preferred_element_type=jnp.float32
        )
        grad_buf[k] = lax.dot_general(
            portion[...], weight, (((1,), (1,)), ((), ())), preferred_element_type=jnp.float32
        ).astype(jnp.bfloat16)
        send(grad_buf.at[k], grad_out.at[:, span])
        value = anchor[span, :]
        fresh = value - (weight.astype(jnp.float32) - inner_rate * grad_weight)
        fresh_buf[k] = fresh.astype(jnp.bfloat16)
        send(fresh_buf.at[k], fresh_out.at[span, :])
        base = value - outer_rate * (
            outer_momentum * outer_momentum * momentum[span, :]
            + (fresh - stale[span, :].astype(jnp.float32)) / workers
        )
        if finish:
            param_buf[k] = finished(kinds[k][0], workers, base, sums[k])
            send(param_buf.at[k], param_out.at[span, :])
        else:
            bases[k][...] = base
    for copy in departures:
        copy.wait()


def finished(kind, workers, base, piece):
    total = piece[...]
    if kind != "own":
        total = decode(total, workers)
    return (base - (outer_rate * (1.0 + outer_momentum) / workers) * total).astype(jnp.bfloat16)


def update_kernel(workers, kinds, me_ref, *rest):
    count = len(kinds)
    bases, pieces, (_, out, out_buf, sem) = rest[:count], rest[count : 2 * count], rest[2 * count :]
    size = out.shape[0] // workers
    known = spots(me_ref[0])
    copies = []
    for k, (kind, sub) in enumerate(kinds):
        out_buf[k] = finished(kind, workers, bases[k][...], pieces[k])
        copies.append(pltpu.make_async_copy(out_buf.at[k], rows(out, block(*known[kind], sub), size), sem.at[k]))
        copies[-1].start()
    for copy in copies:
        copy.wait()


def fast(tokens, inner_weight, key_grad, anchor, momentum, stale_delta):
    workers, shards = lax.axis_size("worker"), lax.axis_size("fsdp")
    f32, bf16 = jnp.float32, jnp.bfloat16
    DMA = pltpu.SemaphoreType.DMA
    weights, stale = inner_weight[0], stale_delta[0]
    height, columns = stale.shape
    batch = tokens.shape[0]
    size = height // workers
    me = jnp.stack([lax.axis_index("worker"), lax.axis_index("fsdp")]).astype(jnp.int32)
    window = (size, columns)

    def swap(value, flips):
        return lax.ppermute(value, "worker", [(i, i ^ flips[i % 2]) for i in range(workers)])

    def across_shards(value, distance):
        return lax.ppermute(value, "fsdp", [(i, i ^ distance) for i in range(shards)])

    beside, first, last = (1, 1), (2, 4), (4, 2)
    chunks = range(2)

    key_rows = batch // shards
    other = swap(stale, beside)
    grad_near = across_shards(key_grad, 1)
    block_of_keys = (key_rows, columns)
    sent, own_keys, later_keys = call(
        keys_kernel,
        [(me, SMEM), (tokens, VMEM), (weights, VMEM)],
        [((2 * key_rows, columns), f32, VMEM), (block_of_keys, f32, VMEM), (block_of_keys, f32, VMEM)],
        scratch=[pltpu.VMEM((batch, columns), f32)],
        micros=0.8,
    )

    codes, keeps = [], []
    for c in chunks:
        code, keep = call(
            functools.partial(pair_kernel, size, c),
            [(me, SMEM), (stale, VMEM), (other, VMEM)],
            [(window, bf16, VMEM), (window, f32, VMEM)],
            after=[sent, grad_near] if c == 0 else [keeps[0]],
            micros=0.9,
        )
        codes.append(code)
        keeps.append(keep)
    got = [swap(codes[c], first) for c in chunks]

    key_near = across_shards(sent, 1)
    grads = [key_grad, grad_near, across_shards(key_grad, 2), across_shards(grad_near, 2)]

    def added(held, total, after):
        for c in chunks:
            keeps[c], codes[c] = call(
                functools.partial(add_kernel, held, total),
                [(keeps[c], VMEM), (got[c], VMEM)],
                [(window, f32, VMEM), (window, bf16, VMEM)],
                after=after if c == 0 else [keeps[0], *after],
                micros=0.5,
            )

    def fresh(kinds, after, finish=None):
        n = len(kinds)
        ins = [(me, SMEM), (tokens, VMEM), (weights, VMEM), (anchor, VMEM), (momentum, VMEM), (stale, VMEM)]
        ins += [(g, VMEM) for g in grads]
        outs = [((height, columns), bf16, HBM), ((batch, height), bf16, HBM)]
        scratch = [
            pltpu.VMEM((batch, columns), bf16),
            pltpu.VMEM((n, *window), bf16),
            pltpu.VMEM((n, batch, size), bf16),
            DMA((3 * n + 2,)),
        ]
        aliases = {}
        if finish is None:
            outs += [(window, f32, VMEM)] * n
        else:
            sums, filled = finish
            ins += [(p, VMEM) for p in [*sums, own_keys, key_far]]
            aliases = {len(ins) + k: k for k in range(2)}
            ins += [(o, HBM) for o in filled]
            outs += [((height, columns), bf16, HBM), (window, f32, HBM), ((key_rows, columns), bf16, HBM)]
            scratch = [
                pltpu.VMEM((n, *window), bf16),
                pltpu.VMEM(window, f32),
                pltpu.VMEM((key_rows, columns), bf16),
            ] + scratch
        return call(
            functools.partial(fresh_kernel, shards, workers, kinds, finish is not None),
            ins,
            outs,
            scratch=scratch,
            after=after,
            aliases=aliases,
            micros=3.0,
        )

    added(2, 4, [])
    got = [swap(codes[c], last) for c in chunks]
    late_kinds = [("near", 0), ("far", 0), ("near", 1), ("far", 1)]
    own_keys, later_keys = call(
        keys_add_kernel,
        [(key_near, VMEM), (own_keys, VMEM), (later_keys, VMEM)],
        [(block_of_keys, f32, VMEM), (block_of_keys, f32, VMEM)],
        after=[keeps[1]],
        micros=0.4,
    )
    key_far = across_shards(later_keys, 2)
    fresh_out, grad_input, *bases = fresh(late_kinds, [keeps[1]])
    added(4, 8, [bases[0]])
    near = [swap(codes[c], first) for c in chunks]
    across = [swap(codes[c], beside) for c in chunks]
    far = [swap(near[c], beside) for c in chunks]
    soon_kinds = [("own", 0), ("own", 1), ("across", 0), ("across", 1)]
    fresh_out, grad_input, updated, new_moment, key_out = fresh(
        soon_kinds, [], ([*keeps, *across], [fresh_out, grad_input])
    )

    for which in ((0, 1, 2), (3,)):
        kinds = [late_kinds[w] for w in which]
        pieces = [near[0], far[0], near[1], far[1]]
        ins = [(me, SMEM)] + [(bases[w], VMEM) for w in which] + [(pieces[w], VMEM) for w in which] + [(updated, HBM)]
        (updated,) = call(
            functools.partial(update_kernel, workers, kinds),
            ins,
            [((height, columns), bf16, HBM)],
            scratch=[pltpu.VMEM((len(which), *window), bf16), DMA((len(which),))],
            aliases={len(ins) - 1: 0},
            micros=1.8,
        )
    return key_out, grad_input, updated[None], new_moment, fresh_out[None]


def plain(tokens, inner_weight, key_grad, anchor, momentum, stale_delta):
    weights = inner_weight[0]
    key_out = lax.psum_scatter(
        jnp.dot(tokens, weights, preferred_element_type=jnp.float32), "fsdp", scatter_dimension=0, tiled=True
    ).astype(jnp.bfloat16)
    portion = lax.all_gather(key_grad, "fsdp", axis=0, tiled=True)
    grad_weight = lax.dot_general(tokens, portion, (((0,), (0,)), ((), ())), preferred_element_type=jnp.float32)
    grad_input = lax.dot_general(portion, weights, (((1,), (1,)), ((), ())), preferred_element_type=jnp.float32)
    fresh_term = anchor - (weights.astype(jnp.float32) - inner_rate * grad_weight)
    stale_value = stale_delta[0].astype(jnp.float32)
    workers = lax.axis_size("worker")
    average = lax.psum(stale_value, "worker") / workers
    moment_full = outer_momentum * momentum + average
    common_term = average + outer_momentum * moment_full
    share_rows = anchor.shape[0] // workers
    new_moment = lax.dynamic_slice_in_dim(moment_full, lax.axis_index("worker") * share_rows, share_rows, 0)
    updated = anchor - outer_rate * (common_term + (fresh_term - stale_value) / workers)
    return (
        key_out,
        grad_input.astype(jnp.bfloat16),
        updated[None].astype(jnp.bfloat16),
        new_moment,
        fresh_term[None].astype(jnp.bfloat16),
    )


def local(*args):
    tokens, inner_weight = args[:2]
    workers, shards = lax.axis_size("worker"), lax.axis_size("fsdp")
    size = inner_weight.shape[1] // workers
    fits = workers == 2**3 and shards == 2**2
    fits = fits and size % 128 == 0 and tokens.shape[0] // shards % 16 == 0
    return (fast if fits else plain)(*args)


def solution(mesh):
    in_specs = (
        P("worker", "fsdp"),
        P("worker", "fsdp", None),
        P(("worker", "fsdp"), None),
        P("fsdp", None),
        P("fsdp", None),
        P("worker", "fsdp", None),
    )
    out_specs = (
        P(("worker", "fsdp"), None),
        P("worker", "fsdp"),
        P("worker", "fsdp", None),
        P(("fsdp", "worker"), None),
        P("worker", "fsdp", None),
    )
    return jax.shard_map(local, mesh=mesh, in_specs=in_specs, out_specs=out_specs, check_vma=False)
```

```python
import functools
import math

import jax
import jax.numpy as jnp
from jax import lax
from jax.experimental import pallas as pl
from jax.experimental.pallas import tpu as pltpu
from jax.sharding import PartitionSpec as P

inner_rate = 0.0005
outer_rate = 0.7
outer_momentum = 0.9

stale_bound = 0.29882812
floor = 2.0**-14
power = 250.0 / math.log2(1.0 + stale_bound / floor)


def encode(value, count):
    grown = jnp.log(jnp.abs(value) * (1.0 / (floor * count)) + 1.0)
    code = jnp.exp2(grown * (power / math.log(2.0)) - 125.0)
    return jnp.where(value < 0, -code, code).astype(jnp.bfloat16)


def decode(code, count):
    code = code.astype(jnp.float32)
    grown = jnp.exp2(jnp.log(jnp.abs(code)) * (1.0 / (power * math.log(2.0))) + 125.0 / power)
    value = (grown - 1.0) * (floor * count)
    return jnp.where(code < 0, -value, value)


pace = 3.3e9
cost = {"pair": (0.9, 0.9), "keys": 0.1, "add": (0.5, 0.5), "keys_add": 0.4, "fresh": (0.5, 3.0), "update": (8.0, 8.0), "relay": 0.3}
opt = {"kg_gate": 0, "keys_at": 2, "keys_gate": 1, "fresh_gate": 1, "add_gate": 3}


def place(me):
    core, low, high = me % 2, (me // 2) % 2, me // 4
    return core, jnp.where(core == 0, low, high), jnp.where(core == 0, high, low)


def block(region, half, sub):
    return jnp.where(region == 0, 4 * sub + 2 * half, 4 * half + 2 * sub + 1)


SMEM, VMEM, HBM, ANY = pltpu.SMEM, pltpu.VMEM, pltpu.HBM, pl.ANY


def call(kernel, ins, outs, scratch=(), after=(), aliases=None, micros=1.0, vmem=12):
    late = len(after)

    def body(*refs):
        kernel(*refs[: len(ins)], *refs[len(ins) + late :])

    def placed(array, space):
        return pltpu.with_memory_space_constraint(array, space) if space in (HBM, VMEM) else array

    return pl.pallas_call(
        body,
        in_specs=[pl.BlockSpec(memory_space=s) for _, s in ins] + [pl.BlockSpec(memory_space=ANY)] * late,
        out_specs=[pl.BlockSpec(memory_space=s) for _, _, s in outs],
        out_shape=[s(shape, dtype) for shape, dtype, s in outs],
        scratch_shapes=scratch,
        input_output_aliases=aliases or {},
        cost_estimate=pl.CostEstimate(flops=int(micros * pace), bytes_accessed=0, transcendentals=0),
        compiler_params=pltpu.CompilerParams(vmem_limit_bytes=vmem * 2**20),
    )(*[placed(a, s) for a, s in ins], *after)


def rows(ref, at, size):
    return ref.at[pl.ds(pl.multiple_of(at * size, size), size), :]


def pair_sums(size, own, other, places, code, keep):
    step = 64

    def summed(k, at):
        there = pl.ds(pl.multiple_of(places[k] * size + at, step), step)
        return own[k * size + at : k * size + at + step, :].astype(jnp.float32) + other[there, :].astype(jnp.float32)

    for at in range(0, size, step):
        code[at : at + step, :] = encode(summed(0, at), 2)
        keep[at : at + step, :] = summed(1, at)


def first_pair_kernel(size, stale, other, code, keep, next_own, own, sem):
    core, first, _ = place(lax.axis_index("worker"))
    places = [[block(core, half, sub) for half in (1 - first, first)] for sub in range(2)]
    copies = [
        pltpu.make_async_copy(rows(stale, at, size), target.at[k * size : (k + 1) * size, :], sem.at[2 * sub + k])
        for sub, target in enumerate((own, next_own))
        for k, at in enumerate(places[sub])
    ]
    for copy in copies:
        copy.start()
    for copy in copies[:2]:
        copy.wait()
    pair_sums(size, own, other, places[0], code, keep)
    for copy in copies[2:]:
        copy.wait()


def second_pair_kernel(size, own, other, grad, grad_far, code, keep, both):
    core, first, _ = place(lax.axis_index("worker"))
    places = [block(core, half, 1) for half in (1 - first, first)]
    pair_sums(size, own, other, places, code, keep)
    both[: grad.shape[0], :] = grad[...]
    both[grad.shape[0] :, :] = grad_far[...]


def add_kernel(held, total, value, received, out, code):
    summed = value[...] + decode(received[...], held)
    out[...] = summed
    code[...] = encode(summed, total)


def keys_kernel(tokens, weights, sent, own, later, total):
    total[...] = jnp.dot(tokens[...], weights[...], preferred_element_type=jnp.float32)
    size = own.shape[0]
    shard = lax.axis_index("fsdp")
    sent[:size, :] = rows(total, shard ^ 1, size)[...]
    sent[size:, :] = rows(total, shard ^ 3, size)[...]
    own[...] = rows(total, shard, size)[...]
    later[...] = rows(total, shard ^ 2, size)[...]


def keys_add_kernel(received, own, later, own_out, later_out):
    size = own.shape[0]
    own_out[...] = own[...] + received[:size, :]
    later_out[...] = later[...] + received[size:, :]


def relay_kernel(*refs):
    half = len(refs) // 2
    for source, target in zip(refs[:half], refs[half:], strict=True):
        target[...] = source[...]


def spots(me):
    core, first, last = place(me)
    return {
        "own": (core, first),
        "near": (core, 1 - first),
        "across": (1 - core, last),
        "far": (1 - core, 1 - last),
    }


def span_of(size, kind, sub):
    return pl.ds(pl.multiple_of(block(*spots(lax.axis_index("worker"))[kind], sub) * size, size), size)


def fresh_kernel(workers, kinds, before, tokens, weights, anchor, momentum, stale, near, far, *rest):
    count = len(kinds)
    if before:
        sums, early, rest = rest[:count], rest[count : count + 2], rest[count + 2 :]
        fresh_out, grad_out, fresh_buf, grad_buf, param_buf, moment, portion, sem = rest
    else:
        fresh_buf, grad_buf, bases, portion = rest[0], rest[1], rest[2 : 2 + count], rest[2 + count]
    size = weights.shape[0] // workers
    copies = []
    if before:
        for k, which in enumerate(before):
            span = span_of(size, *which)
            copies.append(pltpu.make_async_copy(early[0].at[k], fresh_out.at[span, :], sem.at[2 * k]))
            copies.append(pltpu.make_async_copy(early[1].at[k], grad_out.at[:, span], sem.at[2 * k + 1]))
        for copy in copies:
            copy.start()
        _, _, last = place(lax.axis_index("worker"))
        average = jnp.where(last == 0, sums[0][...], sums[1][...]) / workers
        moment[...] = outer_momentum * rows(momentum, lax.axis_index("worker"), size)[...] + average
    held = near.shape[0] // 2
    shard = lax.axis_index("fsdp")
    for d, source in ((0, near.at[:held, :]), (2, near.at[held:, :]), (1, far.at[:held, :]), (3, far.at[held:, :])):
        rows(portion, shard ^ d, held)[...] = source[...]
    for k, which in enumerate(kinds):
        span = span_of(size, *which)
        weight = weights[span, :]
        grad_weight = lax.dot_general(
            tokens[:, span], portion[...], (((0,), (0,)), ((), ())), preferred_element_type=jnp.float32
        )
        grad_buf[k] = lax.dot_general(
            portion[...], weight, (((1,), (1,)), ((), ())), preferred_element_type=jnp.float32
        ).astype(jnp.bfloat16)
        value = anchor[span, :]
        fresh = value - (weight.astype(jnp.float32) - inner_rate * grad_weight)
        fresh_buf[k] = fresh.astype(jnp.bfloat16)
        base = value - outer_rate * (
            outer_momentum * outer_momentum * momentum[span, :]
            + (fresh - stale[span, :].astype(jnp.float32)) / workers
        )
        if before:
            param_buf[k] = finished(kinds[k][0], workers, base, sums[k])
        else:
            bases[k][...] = base
    for copy in copies:
        copy.wait()


def finished(kind, workers, base, piece):
    total = piece[...]
    if kind != "own":
        total = decode(total, workers)
    return (base - (outer_rate * (1.0 + outer_momentum) / workers) * total).astype(jnp.bfloat16)


def near_kernel(workers, kinds, done, *rest):
    count = len(kinds)
    bases, pieces, (fresh_buf, grad_buf, param_buf, moment), rest = (
        rest[:count],
        rest[count : 2 * count],
        rest[2 * count : 2 * count + 4],
        rest[2 * count + 6 :],
    )
    fresh_out, grad_out, out, moment_out, out_buf, sem = rest
    size = out.shape[0] // workers
    copies = []

    def send(source, target):
        copies.append(pltpu.make_async_copy(source, target, sem.at[len(copies)]))
        copies[-1].start()

    send(moment, moment_out)
    for k, which in enumerate(done):
        span = span_of(size, *which)
        send(fresh_buf.at[k], fresh_out.at[span, :])
        send(grad_buf.at[k], grad_out.at[:, span])
        send(param_buf.at[k], out.at[span, :])
    for k, which in enumerate(kinds):
        out_buf[k] = finished(which[0], workers, bases[k][...], pieces[k])
        send(out_buf.at[k], out.at[span_of(size, *which), :])
    for copy in copies:
        copy.wait()


def far_kernel(workers, kinds, *rest):
    count = len(kinds)
    bases, pieces, rest = rest[:count], rest[count : 2 * count], rest[2 * count :]
    own, received, _, out, key_out, out_buf, key_buf, sem = rest
    size = out.shape[0] // workers
    key_buf[...] = (own[...] + received[...]).astype(jnp.bfloat16)
    copies = [pltpu.make_async_copy(key_buf, key_out, sem.at[count])]
    copies[0].start()
    for k, which in enumerate(kinds):
        out_buf[k] = finished(which[0], workers, bases[k][...], pieces[k])
        copies.append(
            pltpu.make_async_copy(out_buf.at[k], out.at[span_of(size, *which), :], sem.at[k])
        )
        copies[-1].start()
    for copy in copies:
        copy.wait()


def fast(tokens, inner_weight, key_grad, anchor, momentum, stale_delta):
    workers, shards = lax.axis_size("worker"), lax.axis_size("fsdp")
    f32, bf16 = jnp.float32, jnp.bfloat16
    DMA = pltpu.SemaphoreType.DMA
    weights, stale = inner_weight[0], stale_delta[0]
    height, columns = stale.shape
    batch = tokens.shape[0]
    size = height // workers
    window = (size, columns)

    def swap(value, flips):
        return lax.ppermute(value, "worker", [(i, i ^ flips[i % 2]) for i in range(workers)])

    def across_shards(value, distance):
        return lax.ppermute(value, "fsdp", [(i, i ^ distance) for i in range(shards)])

    beside, first, last = (1, 1), (2, 4), (4, 2)
    chunks = range(2)

    key_rows = batch // shards
    other = swap(stale, beside)
    grad_far = across_shards(key_grad, 2)
    block_of_keys = (key_rows, columns)
    sums = [(window, bf16, VMEM), (window, f32, VMEM)]
    first_code, first_keep, next_own = call(
        functools.partial(first_pair_kernel, size),
        [(stale, HBM), (other, VMEM)],
        [*sums, ((2 * size, columns), bf16, VMEM)],
        scratch=[pltpu.VMEM((2 * size, columns), bf16), DMA((4,))],
        micros=cost["pair"][0],
    )
    second_code, second_keep, both = call(
        functools.partial(second_pair_kernel, size),
        [(next_own, VMEM), (other, VMEM), (key_grad, VMEM), (grad_far, VMEM)],
        [*sums, ((2 * key_grad.shape[0], columns), bf16, VMEM)],
        after=[first_keep],
        micros=cost["pair"][1],
    )
    codes, keeps = [first_code, second_code], [first_keep, second_keep]
    got = [swap(codes[c], first) for c in chunks]

    def keys(after):
        return call(
            keys_kernel,
            [(tokens, VMEM), (weights, VMEM)],
            [((2 * key_rows, columns), f32, VMEM), (block_of_keys, f32, VMEM), (block_of_keys, f32, VMEM)],
            scratch=[pltpu.VMEM((batch, columns), f32)],
            after=after,
            micros=cost["keys"],
        )

    grads = [both, across_shards(both, 1)]
    def added(held, total, gates):
        for c in chunks:
            keeps[c], codes[c] = call(
                functools.partial(add_kernel, held, total),
                [(keeps[c], VMEM), (got[c], VMEM)],
                [(window, f32, VMEM), (window, bf16, VMEM)],
                after=gates[c] if c == 0 else [keeps[0], *gates[c]],
                micros=cost["add"][c],
            )

    blocks = (4, size, columns), (4, batch, size)

    def fresh(kinds, after, sums=(), early=(), before=None):
        ins = [(tokens, VMEM), (weights, VMEM), (anchor, VMEM), (momentum, VMEM), (stale, VMEM)]
        ins += [(g, VMEM) for g in [*grads, *sums, *early]]
        outs = [(blocks[0], bf16, VMEM), (blocks[1], bf16, VMEM)]
        scratch = [pltpu.VMEM((batch, columns), bf16)]
        if before is None:
            outs += [(window, f32, VMEM)] * len(kinds)
        else:
            outs = [((height, columns), bf16, HBM), ((batch, height), bf16, HBM), *outs]
            outs += [(blocks[0], bf16, VMEM), (window, f32, VMEM)]
            scratch.append(DMA((2 * len(before),)))
        return call(
            functools.partial(fresh_kernel, workers, kinds, before),
            ins,
            outs,
            scratch=scratch,
            after=after,
            micros=cost["fresh"][0 if before is None else 1],
        )

    late_kinds = [("near", 0), ("far", 0), ("near", 1), ("far", 1)]
    gates = [[], []]
    if opt["keys_at"] == 0:
        sent, own_keys, later_keys = keys([keeps[1]])
        if opt["keys_gate"]:
            gates[opt["keys_gate"] - 1].append(sent)
    if opt["kg_gate"]:
        gates[opt["kg_gate"] - 1].append(grads[1])
    added(2, 4, gates)
    got = [swap(codes[c], last) for c in chunks]
    if opt["keys_at"]:
        sent, own_keys, later_keys = keys([keeps[opt["keys_at"] - 1]])
    key_near = across_shards(sent, 1)
    own_keys, later_keys = call(
        keys_add_kernel,
        [(key_near, VMEM), (own_keys, VMEM), (later_keys, VMEM)],
        [(block_of_keys, f32, VMEM), (block_of_keys, f32, VMEM)],
        after=[keeps[1]],
        micros=cost["keys_add"],
    )
    key_far = across_shards(later_keys, 2)
    *early, base_a, base_b, base_c, base_d = fresh(late_kinds, [keeps[1]])
    bases = [base_a, base_b, base_c, base_d]
    gates = [[], []]
    if opt["fresh_gate"]:
        gates[opt["fresh_gate"] - 1].append(bases[0])
    if opt["add_gate"] in (1, 2):
        gates[opt["add_gate"] - 1].append(own_keys)
    added(4, 8, gates)
    near = [swap(codes[c], first) for c in chunks]
    across = [swap(codes[c], beside) for c in chunks]
    soon_kinds = [("own", 0), ("own", 1), ("across", 0), ("across", 1)]
    fresh_out, grad_input, *done = fresh(
        soon_kinds, [own_keys] if opt["add_gate"] == 3 else [], [*keeps, *across], early, late_kinds
    )
    relayed = call(
        relay_kernel, [(n, VMEM) for n in near], [(window, bf16, VMEM)] * 2, after=[done[2]], micros=cost["relay"]
    )
    far = [swap(n, beside) for n in relayed]

    ins = [(value, VMEM) for value in (bases[0], bases[2], *near, *done)]
    ins += [(fresh_out, HBM), (grad_input, HBM)]
    fresh_out, grad_input, updated, new_moment = call(
        functools.partial(near_kernel, workers, late_kinds[::2], soon_kinds),
        ins,
        [
            ((height, columns), bf16, HBM),
            ((batch, height), bf16, HBM),
            ((height, columns), bf16, HBM),
            (window, f32, HBM),
        ],
        scratch=[pltpu.VMEM((2, *window), bf16), DMA((3 * len(soon_kinds) + 3,))],
        aliases={len(ins) - 2: 0, len(ins) - 1: 1},
        micros=cost["update"][0],
    )
    ins = [(value, VMEM) for value in (bases[1], bases[3], *far, own_keys, key_far)]
    ins.append((updated, HBM))
    updated, key_out = call(
        functools.partial(far_kernel, workers, late_kinds[1::2]),
        ins,
        [((height, columns), bf16, HBM), ((key_rows, columns), bf16, HBM)],
        scratch=[pltpu.VMEM((2, *window), bf16), pltpu.VMEM((key_rows, columns), bf16), DMA((3,))],
        aliases={len(ins) - 1: 0},
        micros=cost["update"][1],
    )
    return key_out, grad_input, updated[None], new_moment, fresh_out[None]


def plain(tokens, inner_weight, key_grad, anchor, momentum, stale_delta):
    weights = inner_weight[0]
    key_out = lax.psum_scatter(
        jnp.dot(tokens, weights, preferred_element_type=jnp.float32), "fsdp", scatter_dimension=0, tiled=True
    ).astype(jnp.bfloat16)
    portion = lax.all_gather(key_grad, "fsdp", axis=0, tiled=True)
    grad_weight = lax.dot_general(tokens, portion, (((0,), (0,)), ((), ())), preferred_element_type=jnp.float32)
    grad_input = lax.dot_general(portion, weights, (((1,), (1,)), ((), ())), preferred_element_type=jnp.float32)
    fresh_term = anchor - (weights.astype(jnp.float32) - inner_rate * grad_weight)
    stale_value = stale_delta[0].astype(jnp.float32)
    workers = lax.axis_size("worker")
    average = lax.psum(stale_value, "worker") / workers
    moment_full = outer_momentum * momentum + average
    common_term = average + outer_momentum * moment_full
    share_rows = anchor.shape[0] // workers
    new_moment = lax.dynamic_slice_in_dim(moment_full, lax.axis_index("worker") * share_rows, share_rows, 0)
    updated = anchor - outer_rate * (common_term + (fresh_term - stale_value) / workers)
    return (
        key_out,
        grad_input.astype(jnp.bfloat16),
        updated[None].astype(jnp.bfloat16),
        new_moment,
        fresh_term[None].astype(jnp.bfloat16),
    )


def local(*args):
    tokens, inner_weight = args[:2]
    workers, shards = lax.axis_size("worker"), lax.axis_size("fsdp")
    size = inner_weight.shape[1] // workers
    fits = workers == 2**3 and shards == 2**2
    fits = fits and size % 128 == 0 and tokens.shape[0] // shards % 16 == 0
    return (fast if fits else plain)(*args)


def solution(mesh):
    in_specs = (
        P("worker", "fsdp"),
        P("worker", "fsdp", None),
        P(("worker", "fsdp"), None),
        P("fsdp", None),
        P("fsdp", None),
        P("worker", "fsdp", None),
    )
    out_specs = (
        P(("worker", "fsdp"), None),
        P("worker", "fsdp"),
        P("worker", "fsdp", None),
        P(("fsdp", "worker"), None),
        P("worker", "fsdp", None),
    )
    return jax.shard_map(local, mesh=mesh, in_specs=in_specs, out_specs=out_specs, check_vma=False)
```

```python
import functools
import math

import jax
import jax.numpy as jnp
from jax import lax
from jax.experimental import pallas as pl
from jax.experimental.pallas import tpu as pltpu
from jax.sharding import PartitionSpec as P

inner_rate = 0.0005
outer_rate = 0.7
outer_momentum = 0.9

stale_bound = 0.29882812
floor = 2.0**-14
power = 250.0 / math.log2(1.0 + stale_bound / floor)


def encode(value, count):
    grown = jnp.log(jnp.abs(value) * (1.0 / (floor * count)) + 1.0)
    code = jnp.exp2(grown * (power / math.log(2.0)) - 125.0)
    return jnp.where(value < 0, -code, code).astype(jnp.bfloat16)


def decode(code, count):
    code = code.astype(jnp.float32)
    grown = jnp.exp2(jnp.log(jnp.abs(code)) * (1.0 / (power * math.log(2.0))) + 125.0 / power)
    value = (grown - 1.0) * (floor * count)
    return jnp.where(code < 0, -value, value)


pace = 3.3e9
cost = {"pair": (0.9, 0.9), "keys": 0.1, "add": (0.5, 0.5), "keys_add": 0.4, "fresh": 0.3, "update": (8.0, 8.0), "relay": 0.3, "fetch": 0.5}
opt = {"kg_gate": 0, "keys_gate": 2, "add_gate": 1}


def place(me):
    core, low, high = me % 2, (me // 2) % 2, me // 4
    return core, jnp.where(core == 0, low, high), jnp.where(core == 0, high, low)


def block(region, half, sub):
    return jnp.where(region == 0, 4 * sub + 2 * half, 4 * half + 2 * sub + 1)


SMEM, VMEM, HBM, ANY = pltpu.SMEM, pltpu.VMEM, pltpu.HBM, pl.ANY


def call(kernel, ins, outs, scratch=(), after=(), aliases=None, micros=1.0, vmem=12):
    late = len(after)

    def body(*refs):
        kernel(*refs[: len(ins)], *refs[len(ins) + late :])

    def placed(array, space):
        return pltpu.with_memory_space_constraint(array, space) if space in (HBM, VMEM) else array

    return pl.pallas_call(
        body,
        in_specs=[pl.BlockSpec(memory_space=s) for _, s in ins] + [pl.BlockSpec(memory_space=ANY)] * late,
        out_specs=[pl.BlockSpec(memory_space=s) for _, _, s in outs],
        out_shape=[s(shape, dtype) for shape, dtype, s in outs],
        scratch_shapes=scratch,
        input_output_aliases=aliases or {},
        cost_estimate=pl.CostEstimate(flops=int(micros * pace), bytes_accessed=0, transcendentals=0),
        compiler_params=pltpu.CompilerParams(vmem_limit_bytes=vmem * 2**20),
    )(*[placed(a, s) for a, s in ins], *after)


def rows(ref, at, size):
    return ref.at[pl.ds(pl.multiple_of(at * size, size), size), :]


def pair_sums(size, own, other, places, code, keep):
    step = 64

    def summed(k, at):
        there = pl.ds(pl.multiple_of(places[k] * size + at, step), step)
        return own[k * size + at : k * size + at + step, :].astype(jnp.float32) + other[there, :].astype(jnp.float32)

    for at in range(0, size, step):
        code[at : at + step, :] = encode(summed(0, at), 2)
        keep[at : at + step, :] = summed(1, at)


def fetch_kernel(size, stale, grad, first_own, second_own, grad_out, sem):
    core, first, _ = place(lax.axis_index("worker"))
    copies = [
        pltpu.make_async_copy(
            rows(stale, block(core, half, sub), size), own.at[k * size : (k + 1) * size, :], sem.at[2 * sub + k]
        )
        for sub, own in enumerate((first_own, second_own))
        for k, half in enumerate((1 - first, first))
    ]
    copies.append(pltpu.make_async_copy(grad, grad_out, sem.at[4]))
    for copy in copies:
        copy.start()
    for copy in copies:
        copy.wait()


def pair_kernel(size, sub, own, other, code, keep):
    core, first, _ = place(lax.axis_index("worker"))
    places = [block(core, half, sub) for half in (1 - first, first)]
    pair_sums(size, own, other, places, code, keep)


def add_kernel(held, total, value, received, out, code):
    summed = value[...] + decode(received[...], held)
    out[...] = summed
    code[...] = encode(summed, total)


def keys_kernel(tokens, weights, grad, grad_far, packed, own, later, total):
    total[...] = jnp.dot(tokens[...], weights[...], preferred_element_type=jnp.float32)
    size = own.shape[0]
    shard = lax.axis_index("fsdp")
    packed[:size, :] = grad[...]
    packed[size : 2 * size, :] = grad_far[...]
    for k, d in enumerate((1, 3)):
        value = rows(total, shard ^ d, size)[...]
        high = value.astype(jnp.bfloat16)
        packed[(2 + k) * size : (3 + k) * size, :] = high
        packed[(4 + k) * size : (5 + k) * size, :] = (value - high.astype(jnp.float32)).astype(jnp.bfloat16)
    own[...] = rows(total, shard, size)[...]
    later[...] = rows(total, shard ^ 2, size)[...]


def keys_add_kernel(received, own, later, own_out, later_out):
    size = own.shape[0]

    def arrived(k):
        high, low = (received[at * size : (at + 1) * size, :].astype(jnp.float32) for at in (2 + k, 4 + k))
        return high + low

    own_out[...] = own[...] + arrived(0)
    later_out[...] = later[...] + arrived(1)


def relay_kernel(*refs):
    half = len(refs) // 2
    for source, target in zip(refs[:half], refs[half:], strict=True):
        target[...] = source[...]


def spots(me):
    core, first, last = place(me)
    return {
        "own": (core, first),
        "near": (core, 1 - first),
        "across": (1 - core, last),
        "far": (1 - core, 1 - last),
    }


def span_of(size, kind, sub):
    return pl.ds(pl.multiple_of(block(*spots(lax.axis_index("worker"))[kind], sub) * size, size), size)


def fresh_kernel(workers, soon, late, tokens, weights, anchor, momentum, stale, near, far, *rest):
    sums, rest = rest[: len(soon)], rest[len(soon) :]
    fresh_out, grad_out, param_out, moment_out, rest = *rest[:4], rest[4:]
    bases, rest = rest[: len(late)], rest[len(late) :]
    fresh_buf, grad_buf, param_buf, moment, portion, sem = rest
    size = weights.shape[0] // workers
    copies = []

    def send(source, target):
        copies.append(pltpu.make_async_copy(source, target, sem.at[len(copies)]))
        copies[-1].start()

    held = portion.shape[0] // 4
    shard = lax.axis_index("fsdp")
    for d, source, k in ((0, near, 0), (2, near, 1), (1, far, 0), (3, far, 1)):
        rows(portion, shard ^ d, held)[...] = source[k * held : (k + 1) * held, :]
    for k, which in enumerate([*late, *soon]):
        span = span_of(size, *which)
        weight = weights[span, :]
        grad_weight = lax.dot_general(
            tokens[:, span], portion[...], (((0,), (0,)), ((), ())), preferred_element_type=jnp.float32
        )
        grad_buf[k] = lax.dot_general(
            portion[...], weight, (((1,), (1,)), ((), ())), preferred_element_type=jnp.float32
        ).astype(jnp.bfloat16)
        send(grad_buf.at[k], grad_out.at[:, span])
        value = anchor[span, :]
        fresh = value - (weight.astype(jnp.float32) - inner_rate * grad_weight)
        fresh_buf[k] = fresh.astype(jnp.bfloat16)
        send(fresh_buf.at[k], fresh_out.at[span, :])
        base = value - outer_rate * (
            outer_momentum * outer_momentum * momentum[span, :]
            + (fresh - stale[span, :].astype(jnp.float32)) / workers
        )
        if k < len(late):
            bases[k][...] = base
        else:
            k -= len(late)
            param_buf[k] = finished(which[0], workers, base, sums[k])
            send(param_buf.at[k], param_out.at[span, :])
        if which is late[-1]:
            _, _, last = place(lax.axis_index("worker"))
            average = jnp.where(last == 0, sums[0][...], sums[1][...]) / workers
            moment[...] = outer_momentum * rows(momentum, lax.axis_index("worker"), size)[...] + average
            send(moment, moment_out)
    for copy in copies:
        copy.wait()


def finished(kind, workers, base, piece):
    total = piece[...]
    if kind != "own":
        total = decode(total, workers)
    return (base - (outer_rate * (1.0 + outer_momentum) / workers) * total).astype(jnp.bfloat16)


def update_kernel(workers, kinds, keys, *rest):
    count = len(kinds)
    bases, pieces, rest = rest[:count], rest[count : 2 * count], rest[2 * count :]
    if keys:
        own, received, _, out, key_out, out_buf, key_buf, sem = rest
    else:
        _, out, out_buf, sem = rest
    size = out.shape[0] // workers
    copies = []
    if keys:
        key_buf[...] = (own[...] + received[...]).astype(jnp.bfloat16)
        copies.append(pltpu.make_async_copy(key_buf, key_out, sem.at[count]))
        copies[0].start()
    for k, which in enumerate(kinds):
        out_buf[k] = finished(which[0], workers, bases[k][...], pieces[k])
        copies.append(pltpu.make_async_copy(out_buf.at[k], out.at[span_of(size, *which), :], sem.at[k]))
        copies[-1].start()
    for copy in copies:
        copy.wait()


def fast(tokens, inner_weight, key_grad, anchor, momentum, stale_delta):
    workers, shards = lax.axis_size("worker"), lax.axis_size("fsdp")
    f32, bf16 = jnp.float32, jnp.bfloat16
    DMA = pltpu.SemaphoreType.DMA
    weights, stale = inner_weight[0], stale_delta[0]
    height, columns = stale.shape
    batch = tokens.shape[0]
    size = height // workers
    window = (size, columns)

    def swap(value, flips):
        return lax.ppermute(value, "worker", [(i, i ^ flips[i % 2]) for i in range(workers)])

    def across_shards(value, distance):
        return lax.ppermute(value, "fsdp", [(i, i ^ distance) for i in range(shards)])

    beside, first, last = (1, 1), (2, 4), (4, 2)
    chunks = range(2)

    key_rows = batch // shards
    other = swap(stale, beside)
    block_of_keys = (key_rows, columns)
    *owns, grad = call(
        functools.partial(fetch_kernel, size),
        [(stale, HBM), (key_grad, HBM)],
        [((2 * size, columns), bf16, VMEM)] * 2 + [(key_grad.shape, bf16, VMEM)],
        scratch=[DMA((5,))],
        micros=cost["fetch"],
    )
    grad_far = across_shards(grad, 2)

    codes, keeps = [], []
    for c in chunks:
        code, keep = call(
            functools.partial(pair_kernel, size, c),
            [(owns[c], VMEM), (other, VMEM)],
            [(window, bf16, VMEM), (window, f32, VMEM)],
            after=keeps + [grad_far] * (c == 1 and opt["kg_gate"]),
            micros=cost["pair"][c],
        )
        codes.append(code)
        keeps.append(keep)
    got = [swap(codes[c], first) for c in chunks]

    packed, own_keys, later_keys = call(
        keys_kernel,
        [(tokens, VMEM), (weights, VMEM), (grad, VMEM), (grad_far, VMEM)],
        [((6 * key_rows, columns), bf16, VMEM), (block_of_keys, f32, VMEM), (block_of_keys, f32, VMEM)],
        scratch=[pltpu.VMEM((batch, columns), f32)],
        after=[keeps[1]],
        micros=cost["keys"],
    )
    arrived = across_shards(packed, 1)
    grads = [packed, arrived]

    def added(held, total, gates):
        for c in chunks:
            keeps[c], codes[c] = call(
                functools.partial(add_kernel, held, total),
                [(keeps[c], VMEM), (got[c], VMEM)],
                [(window, f32, VMEM), (window, bf16, VMEM)],
                after=gates[c] if c == 0 else [keeps[0], *gates[c]],
                micros=cost["add"][c],
            )

    late_kinds = [("near", 0), ("far", 0), ("near", 1), ("far", 1)]
    gates = [[], []]
    if opt["keys_gate"]:
        gates[opt["keys_gate"] - 1].append(packed)
    added(2, 4, gates)
    got = [swap(codes[c], last) for c in chunks]
    own_keys, later_keys = call(
        keys_add_kernel,
        [(arrived, VMEM), (own_keys, VMEM), (later_keys, VMEM)],
        [(block_of_keys, f32, VMEM), (block_of_keys, f32, VMEM)],
        after=[keeps[1]],
        micros=cost["keys_add"],
    )
    key_far = across_shards(later_keys, 2)
    gates = [[], []]
    if opt["add_gate"] in (1, 2):
        gates[opt["add_gate"] - 1].append(own_keys)
    added(4, 8, gates)
    near = [swap(codes[c], first) for c in chunks]
    across = [swap(codes[c], beside) for c in chunks]
    soon_kinds = [("own", 0), ("own", 1), ("across", 0), ("across", 1)]
    late_kinds = [("near", 0), ("near", 1), ("far", 0), ("far", 1)]
    n = len(soon_kinds)
    ins = [tokens, weights, anchor, momentum, stale, packed, arrived, *keeps, *across]
    fresh_out, grad_input, updated, new_moment, *bases = call(
        functools.partial(fresh_kernel, workers, soon_kinds, late_kinds),
        [(value, VMEM) for value in ins],
        [
            ((height, columns), bf16, HBM),
            ((batch, height), bf16, HBM),
            ((height, columns), bf16, HBM),
            (window, f32, HBM),
        ]
        + [(window, f32, VMEM)] * n,
        scratch=[
            pltpu.VMEM((2 * n, *window), bf16),
            pltpu.VMEM((2 * n, batch, size), bf16),
            pltpu.VMEM((n, *window), bf16),
            pltpu.VMEM(window, f32),
            pltpu.VMEM((batch, columns), bf16),
            DMA((5 * n + 1,)),
        ],
        after=[own_keys] if opt["add_gate"] == 3 else [],
        micros=cost["fresh"],
    )
    relayed = call(
        relay_kernel, [(v, VMEM) for v in near], [(window, bf16, VMEM)] * 2, after=[bases[0]], micros=cost["relay"]
    )
    far = [swap(v, beside) for v in relayed]

    pieces = [*near, *far]
    for which, with_keys in (((0, 1), False), ((2, 3), True)):
        ins = [(bases[w], VMEM) for w in which] + [(pieces[w], VMEM) for w in which]
        outs = [((height, columns), bf16, HBM)]
        scratch = [pltpu.VMEM((len(which), *window), bf16)]
        if with_keys:
            ins += [(own_keys, VMEM), (key_far, VMEM)]
            outs.append(((key_rows, columns), bf16, HBM))
            scratch.append(pltpu.VMEM((key_rows, columns), bf16))
        ins.append((updated, HBM))
        updated, *key_out = call(
            functools.partial(update_kernel, workers, [late_kinds[w] for w in which], with_keys),
            ins,
            outs,
            scratch=[*scratch, DMA((len(which) + 1,))],
            aliases={len(ins) - 1: 0},
            micros=cost["update"][with_keys],
        )
    return key_out[0], grad_input, updated[None], new_moment, fresh_out[None]


def plain(tokens, inner_weight, key_grad, anchor, momentum, stale_delta):
    weights = inner_weight[0]
    key_out = lax.psum_scatter(
        jnp.dot(tokens, weights, preferred_element_type=jnp.float32), "fsdp", scatter_dimension=0, tiled=True
    ).astype(jnp.bfloat16)
    portion = lax.all_gather(key_grad, "fsdp", axis=0, tiled=True)
    grad_weight = lax.dot_general(tokens, portion, (((0,), (0,)), ((), ())), preferred_element_type=jnp.float32)
    grad_input = lax.dot_general(portion, weights, (((1,), (1,)), ((), ())), preferred_element_type=jnp.float32)
    fresh_term = anchor - (weights.astype(jnp.float32) - inner_rate * grad_weight)
    stale_value = stale_delta[0].astype(jnp.float32)
    workers = lax.axis_size("worker")
    average = lax.psum(stale_value, "worker") / workers
    moment_full = outer_momentum * momentum + average
    common_term = average + outer_momentum * moment_full
    share_rows = anchor.shape[0] // workers
    new_moment = lax.dynamic_slice_in_dim(moment_full, lax.axis_index("worker") * share_rows, share_rows, 0)
    updated = anchor - outer_rate * (common_term + (fresh_term - stale_value) / workers)
    return (
        key_out,
        grad_input.astype(jnp.bfloat16),
        updated[None].astype(jnp.bfloat16),
        new_moment,
        fresh_term[None].astype(jnp.bfloat16),
    )


def local(*args):
    tokens, inner_weight = args[:2]
    workers, shards = lax.axis_size("worker"), lax.axis_size("fsdp")
    size = inner_weight.shape[1] // workers
    fits = workers == 2**3 and shards == 2**2
    fits = fits and size % 128 == 0 and tokens.shape[0] // shards % 16 == 0
    return (fast if fits else plain)(*args)


def solution(mesh):
    in_specs = (
        P("worker", "fsdp"),
        P("worker", "fsdp", None),
        P(("worker", "fsdp"), None),
        P("fsdp", None),
        P("fsdp", None),
        P("worker", "fsdp", None),
    )
    out_specs = (
        P(("worker", "fsdp"), None),
        P("worker", "fsdp"),
        P("worker", "fsdp", None),
        P(("fsdp", "worker"), None),
        P("worker", "fsdp", None),
    )
    return jax.shard_map(local, mesh=mesh, in_specs=in_specs, out_specs=out_specs, check_vma=False)
```

```python
import functools
import math

import jax
import jax.numpy as jnp
from jax import lax
from jax.experimental import pallas as pl
from jax.experimental.pallas import tpu as pltpu
from jax.sharding import PartitionSpec as P

inner_rate = 0.0005
outer_rate = 0.7
outer_momentum = 0.9

stale_bound = 0.29882812
floor = 2.0**-14
power = 250.0 / math.log2(1.0 + stale_bound / floor)


def encode(value, count):
    grown = jnp.log(jnp.abs(value) * (1.0 / (floor * count)) + 1.0)
    code = jnp.exp2(grown * (power / math.log(2.0)) - 125.0)
    return jnp.where(value < 0, -code, code).astype(jnp.bfloat16)


def decode(code, count):
    code = code.astype(jnp.float32)
    grown = jnp.exp2(jnp.log(jnp.abs(code)) * (1.0 / (power * math.log(2.0))) + 125.0 / power)
    value = (grown - 1.0) * (floor * count)
    return jnp.where(code < 0, -value, value)


pace = 2e9
cost = {
    "fetch": 0.5,
    "pair": (0.9, 0.9),
    "keys": 0.1,
    "add": (0.5, 0.5),
    "keys_add": 0.4,
    "fresh": 0.3,
    "relay": 0.3,
    "update": (8.0, 8.0),
}


def place(me):
    core, low, high = me % 2, (me // 2) % 2, me // 4
    return core, jnp.where(core == 0, low, high), jnp.where(core == 0, high, low)


def block(region, half, sub):
    return jnp.where(region == 0, 4 * sub + 2 * half, 4 * half + 2 * sub + 1)


SMEM, VMEM, HBM, ANY = pltpu.SMEM, pltpu.VMEM, pltpu.HBM, pl.ANY


def call(kernel, ins, outs, scratch=(), after=(), aliases=None, micros=1.0, vmem=12):
    late = len(after)

    def body(*refs):
        kernel(*refs[: len(ins)], *refs[len(ins) + late :])

    def placed(array, space):
        return pltpu.with_memory_space_constraint(array, space) if space in (HBM, VMEM) else array

    return pl.pallas_call(
        body,
        in_specs=[pl.BlockSpec(memory_space=s) for _, s in ins] + [pl.BlockSpec(memory_space=ANY)] * late,
        out_specs=[pl.BlockSpec(memory_space=s) for _, _, s in outs],
        out_shape=[s(shape, dtype) for shape, dtype, s in outs],
        scratch_shapes=scratch,
        input_output_aliases=aliases or {},
        cost_estimate=pl.CostEstimate(flops=int(micros * pace), bytes_accessed=0, transcendentals=0),
        compiler_params=pltpu.CompilerParams(vmem_limit_bytes=vmem * 2**20),
    )(*[placed(a, s) for a, s in ins], *after)


def rows(ref, at, size):
    return ref.at[pl.ds(pl.multiple_of(at * size, size), size), :]


def pair_sums(size, own, other, places, code, keep):
    step = 64

    def summed(k, at):
        there = pl.ds(pl.multiple_of(places[k] * size + at, step), step)
        return own[k * size + at : k * size + at + step, :].astype(jnp.float32) + other[there, :].astype(jnp.float32)

    for at in range(0, size, step):
        code[at : at + step, :] = encode(summed(0, at), 2)
        keep[at : at + step, :] = summed(1, at)


def fetch_kernel(size, stale, grad, first_own, second_own, grad_out, sem):
    core, first, _ = place(lax.axis_index("worker"))
    copies = [
        pltpu.make_async_copy(
            rows(stale, block(core, half, sub), size), own.at[k * size : (k + 1) * size, :], sem.at[2 * sub + k]
        )
        for sub, own in enumerate((first_own, second_own))
        for k, half in enumerate((1 - first, first))
    ]
    copies.append(pltpu.make_async_copy(grad, grad_out, sem.at[4]))
    for copy in copies:
        copy.start()
    for copy in copies:
        copy.wait()


def pair_kernel(size, sub, own, other, code, keep):
    core, first, _ = place(lax.axis_index("worker"))
    places = [block(core, half, sub) for half in (1 - first, first)]
    pair_sums(size, own, other, places, code, keep)


def add_kernel(held, total, value, received, out, code):
    summed = value[...] + decode(received[...], held)
    out[...] = summed
    code[...] = encode(summed, total)


def keys_kernel(tokens, weights, grad, grad_far, packed, own, later, total):
    total[...] = jnp.dot(tokens[...], weights[...], preferred_element_type=jnp.float32)
    size = own.shape[0]
    shard = lax.axis_index("fsdp")
    packed[:size, :] = grad[...]
    packed[size : 2 * size, :] = grad_far[...]
    for k, d in enumerate((1, 3)):
        value = rows(total, shard ^ d, size)[...]
        high = value.astype(jnp.bfloat16)
        packed[(2 + k) * size : (3 + k) * size, :] = high
        packed[(4 + k) * size : (5 + k) * size, :] = (value - high.astype(jnp.float32)).astype(jnp.bfloat16)
    own[...] = rows(total, shard, size)[...]
    later[...] = rows(total, shard ^ 2, size)[...]


def keys_add_kernel(received, own, later, own_out, later_out):
    size = own.shape[0]

    def arrived(k):
        high, low = (received[at * size : (at + 1) * size, :].astype(jnp.float32) for at in (2 + k, 4 + k))
        return high + low

    own_out[...] = own[...] + arrived(0)
    later_out[...] = later[...] + arrived(1)


def relay_kernel(*refs):
    half = len(refs) // 2
    for source, target in zip(refs[:half], refs[half:], strict=True):
        target[...] = source[...]


def spots(me):
    core, first, last = place(me)
    return {
        "own": (core, first),
        "near": (core, 1 - first),
        "across": (1 - core, last),
        "far": (1 - core, 1 - last),
    }


def span_of(size, kind, sub):
    return pl.ds(pl.multiple_of(block(*spots(lax.axis_index("worker"))[kind], sub) * size, size), size)


def fresh_kernel(workers, soon, late, tokens, weights, anchor, momentum, stale, near, far, *rest):
    sums, rest = rest[: len(soon)], rest[len(soon) :]
    fresh_out, grad_out, param_out, moment_out, rest = *rest[:4], rest[4:]
    bases, rest = rest[: len(late)], rest[len(late) :]
    fresh_buf, grad_buf, param_buf, moment, portion, sem = rest
    size = weights.shape[0] // workers
    copies = []

    def send(source, target):
        copies.append(pltpu.make_async_copy(source, target, sem.at[len(copies)]))
        copies[-1].start()

    held = portion.shape[0] // 4
    shard = lax.axis_index("fsdp")
    for d, source, k in ((0, near, 0), (2, near, 1), (1, far, 0), (3, far, 1)):
        rows(portion, shard ^ d, held)[...] = source[k * held : (k + 1) * held, :]
    for k, which in enumerate([*late, *soon]):
        span = span_of(size, *which)
        weight = weights[span, :]
        grad_weight = lax.dot_general(
            tokens[:, span], portion[...], (((0,), (0,)), ((), ())), preferred_element_type=jnp.float32
        )
        grad_buf[k] = lax.dot_general(
            portion[...], weight, (((1,), (1,)), ((), ())), preferred_element_type=jnp.float32
        ).astype(jnp.bfloat16)
        send(grad_buf.at[k], grad_out.at[:, span])
        value = anchor[span, :]
        fresh = value - (weight.astype(jnp.float32) - inner_rate * grad_weight)
        fresh_buf[k] = fresh.astype(jnp.bfloat16)
        send(fresh_buf.at[k], fresh_out.at[span, :])
        base = value - outer_rate * (
            outer_momentum * outer_momentum * momentum[span, :]
            + (fresh - stale[span, :].astype(jnp.float32)) / workers
        )
        if k < len(late):
            bases[k][...] = base
        else:
            k -= len(late)
            param_buf[k] = finished(which[0], workers, base, sums[k])
            send(param_buf.at[k], param_out.at[span, :])
        if which is late[-1]:
            _, _, last = place(lax.axis_index("worker"))
            average = jnp.where(last == 0, sums[0][...], sums[1][...]) / workers
            moment[...] = outer_momentum * rows(momentum, lax.axis_index("worker"), size)[...] + average
            send(moment, moment_out)
    for copy in copies:
        copy.wait()


def finished(kind, workers, base, piece):
    total = piece[...]
    if kind != "own":
        total = decode(total, workers)
    return (base - (outer_rate * (1.0 + outer_momentum) / workers) * total).astype(jnp.bfloat16)


def update_kernel(workers, kinds, keys, *rest):
    count = len(kinds)
    bases, pieces, rest = rest[:count], rest[count : 2 * count], rest[2 * count :]
    if keys:
        own, received, _, out, key_out, out_buf, key_buf, sem = rest
    else:
        _, out, out_buf, sem = rest
    size = out.shape[0] // workers
    copies = []
    if keys:
        key_buf[...] = (own[...] + received[...]).astype(jnp.bfloat16)
        copies.append(pltpu.make_async_copy(key_buf, key_out, sem.at[count]))
        copies[0].start()
    for k, which in enumerate(kinds):
        out_buf[k] = finished(which[0], workers, bases[k][...], pieces[k])
        copies.append(pltpu.make_async_copy(out_buf.at[k], out.at[span_of(size, *which), :], sem.at[k]))
        copies[-1].start()
    for copy in copies:
        copy.wait()


def fast(tokens, inner_weight, key_grad, anchor, momentum, stale_delta):
    workers, shards = lax.axis_size("worker"), lax.axis_size("fsdp")
    f32, bf16 = jnp.float32, jnp.bfloat16
    DMA = pltpu.SemaphoreType.DMA
    weights, stale = inner_weight[0], stale_delta[0]
    height, columns = stale.shape
    batch = tokens.shape[0]
    size = height // workers
    window = (size, columns)

    def swap(value, flips):
        return lax.ppermute(value, "worker", [(i, i ^ flips[i % 2]) for i in range(workers)])

    def across_shards(value, distance):
        return lax.ppermute(value, "fsdp", [(i, i ^ distance) for i in range(shards)])

    beside, first, last = (1, 1), (2, 4), (4, 2)
    chunks = range(2)

    key_rows = batch // shards
    other = swap(stale, beside)
    block_of_keys = (key_rows, columns)
    *owns, grad = call(
        functools.partial(fetch_kernel, size),
        [(stale, HBM), (key_grad, HBM)],
        [((2 * size, columns), bf16, VMEM)] * 2 + [(key_grad.shape, bf16, VMEM)],
        scratch=[DMA((5,))],
        micros=cost["fetch"],
    )
    grad_far = across_shards(grad, 2)

    codes, keeps = [], []
    for c in chunks:
        code, keep = call(
            functools.partial(pair_kernel, size, c),
            [(owns[c], VMEM), (other, VMEM)],
            [(window, bf16, VMEM), (window, f32, VMEM)],
            after=keeps,
            micros=cost["pair"][c],
        )
        codes.append(code)
        keeps.append(keep)
    got = [swap(codes[c], first) for c in chunks]

    packed, own_keys, later_keys = call(
        keys_kernel,
        [(tokens, VMEM), (weights, VMEM), (grad, VMEM), (grad_far, VMEM)],
        [((6 * key_rows, columns), bf16, VMEM), (block_of_keys, f32, VMEM), (block_of_keys, f32, VMEM)],
        scratch=[pltpu.VMEM((batch, columns), f32)],
        after=[keeps[1]],
        micros=cost["keys"],
    )
    arrived = across_shards(packed, 1)
    grads = [packed, arrived]

    def added(held, total, before_second):
        for c in chunks:
            keeps[c], codes[c] = call(
                functools.partial(add_kernel, held, total),
                [(keeps[c], VMEM), (got[c], VMEM)],
                [(window, f32, VMEM), (window, bf16, VMEM)],
                after=[] if c == 0 else [keeps[0], *before_second],
                micros=cost["add"][c],
            )

    late_kinds = [("near", 0), ("far", 0), ("near", 1), ("far", 1)]
    added(2, 4, [packed])
    got = [swap(codes[c], last) for c in chunks]
    own_keys, later_keys = call(
        keys_add_kernel,
        [(arrived, VMEM), (own_keys, VMEM), (later_keys, VMEM)],
        [(block_of_keys, f32, VMEM), (block_of_keys, f32, VMEM)],
        after=[keeps[1]],
        micros=cost["keys_add"],
    )
    key_far = across_shards(later_keys, 2)
    added(4, 8, [own_keys])
    near = [swap(codes[c], first) for c in chunks]
    across = [swap(codes[c], beside) for c in chunks]
    soon_kinds = [("own", 0), ("own", 1), ("across", 0), ("across", 1)]
    late_kinds = [("near", 0), ("near", 1), ("far", 0), ("far", 1)]
    n = len(soon_kinds)
    ins = [tokens, weights, anchor, momentum, stale, packed, arrived, *keeps, *across]
    fresh_out, grad_input, updated, new_moment, *bases = call(
        functools.partial(fresh_kernel, workers, soon_kinds, late_kinds),
        [(value, VMEM) for value in ins],
        [
            ((height, columns), bf16, HBM),
            ((batch, height), bf16, HBM),
            ((height, columns), bf16, HBM),
            (window, f32, HBM),
        ]
        + [(window, f32, VMEM)] * n,
        scratch=[
            pltpu.VMEM((2 * n, *window), bf16),
            pltpu.VMEM((2 * n, batch, size), bf16),
            pltpu.VMEM((n, *window), bf16),
            pltpu.VMEM(window, f32),
            pltpu.VMEM((batch, columns), bf16),
            DMA((5 * n + 1,)),
        ],
        micros=cost["fresh"],
    )
    relayed = call(
        relay_kernel, [(v, VMEM) for v in near], [(window, bf16, VMEM)] * 2, after=[bases[0]], micros=cost["relay"]
    )
    far = [swap(v, beside) for v in relayed]

    pieces = [*near, *far]
    for which, with_keys in (((0, 1), False), ((2, 3), True)):
        ins = [(bases[w], VMEM) for w in which] + [(pieces[w], VMEM) for w in which]
        outs = [((height, columns), bf16, HBM)]
        scratch = [pltpu.VMEM((len(which), *window), bf16)]
        if with_keys:
            ins += [(own_keys, VMEM), (key_far, VMEM)]
            outs.append(((key_rows, columns), bf16, HBM))
            scratch.append(pltpu.VMEM((key_rows, columns), bf16))
        ins.append((updated, HBM))
        updated, *key_out = call(
            functools.partial(update_kernel, workers, [late_kinds[w] for w in which], with_keys),
            ins,
            outs,
            scratch=[*scratch, DMA((len(which) + 1,))],
            aliases={len(ins) - 1: 0},
            micros=cost["update"][with_keys],
        )
    return key_out[0], grad_input, updated[None], new_moment, fresh_out[None]


def plain(tokens, inner_weight, key_grad, anchor, momentum, stale_delta):
    weights = inner_weight[0]
    key_out = lax.psum_scatter(
        jnp.dot(tokens, weights, preferred_element_type=jnp.float32), "fsdp", scatter_dimension=0, tiled=True
    ).astype(jnp.bfloat16)
    portion = lax.all_gather(key_grad, "fsdp", axis=0, tiled=True)
    grad_weight = lax.dot_general(tokens, portion, (((0,), (0,)), ((), ())), preferred_element_type=jnp.float32)
    grad_input = lax.dot_general(portion, weights, (((1,), (1,)), ((), ())), preferred_element_type=jnp.float32)
    fresh_term = anchor - (weights.astype(jnp.float32) - inner_rate * grad_weight)
    stale_value = stale_delta[0].astype(jnp.float32)
    workers = lax.axis_size("worker")
    average = lax.psum(stale_value, "worker") / workers
    moment_full = outer_momentum * momentum + average
    common_term = average + outer_momentum * moment_full
    share_rows = anchor.shape[0] // workers
    new_moment = lax.dynamic_slice_in_dim(moment_full, lax.axis_index("worker") * share_rows, share_rows, 0)
    updated = anchor - outer_rate * (common_term + (fresh_term - stale_value) / workers)
    return (
        key_out,
        grad_input.astype(jnp.bfloat16),
        updated[None].astype(jnp.bfloat16),
        new_moment,
        fresh_term[None].astype(jnp.bfloat16),
    )


def local(*args):
    tokens, inner_weight = args[:2]
    workers, shards = lax.axis_size("worker"), lax.axis_size("fsdp")
    size = inner_weight.shape[1] // workers
    fits = workers == 2**3 and shards == 2**2
    fits = fits and size % 128 == 0 and tokens.shape[0] // shards % 16 == 0
    return (fast if fits else plain)(*args)


def solution(mesh):
    in_specs = (
        P("worker", "fsdp"),
        P("worker", "fsdp", None),
        P(("worker", "fsdp"), None),
        P("fsdp", None),
        P("fsdp", None),
        P("worker", "fsdp", None),
    )
    out_specs = (
        P(("worker", "fsdp"), None),
        P("worker", "fsdp"),
        P("worker", "fsdp", None),
        P(("fsdp", "worker"), None),
        P("worker", "fsdp", None),
    )
    return jax.shard_map(local, mesh=mesh, in_specs=in_specs, out_specs=out_specs, check_vma=False)
```

```python
import functools
import math

import jax
import jax.numpy as jnp
from jax import lax
from jax.experimental import pallas as pl
from jax.experimental.pallas import tpu as pltpu
from jax.sharding import PartitionSpec as P

inner_rate = 0.0005
outer_rate = 0.7
outer_momentum = 0.9

stale_bound = 0.29882812
floor = 2.0**-14
power = 250.0 / math.log2(1.0 + stale_bound / floor)


def encode(value, count):
    grown = jnp.log(jnp.abs(value) * (1.0 / (floor * count)) + 1.0)
    code = jnp.exp2(grown * (power / math.log(2.0)) - 125.0)
    return jnp.where(value < 0, -code, code).astype(jnp.bfloat16)


def decode(code, count):
    code = code.astype(jnp.float32)
    grown = jnp.exp2(jnp.log(jnp.abs(code)) * (1.0 / (power * math.log(2.0))) + 125.0 / power)
    value = (grown - 1.0) * (floor * count)
    return jnp.where(code < 0, -value, value)


pace = 2e9
cost = {
    "fetch": 0.5,
    "pair": (0.9, 0.9),
    "keys": 0.1,
    "add": (0.5, 0.5),
    "keys_add": 0.4,
    "fresh": 0.3,
    "relay": 0.3,
    "update": (8.0, 8.0),
}


def place(me):
    core, low, high = me % 2, (me // 2) % 2, me // 4
    return core, jnp.where(core == 0, low, high), jnp.where(core == 0, high, low)


def block(region, half, sub):
    return jnp.where(region == 0, 4 * sub + 2 * half, 4 * half + 2 * sub + 1)


SMEM, VMEM, HBM, ANY = pltpu.SMEM, pltpu.VMEM, pltpu.HBM, pl.ANY


def call(kernel, ins, outs, scratch=(), after=(), aliases=None, micros=1.0, vmem=12):
    late = len(after)

    def body(*refs):
        kernel(*refs[: len(ins)], *refs[len(ins) + late :])

    def placed(array, space):
        return pltpu.with_memory_space_constraint(array, space) if space in (HBM, VMEM) else array

    return pl.pallas_call(
        body,
        in_specs=[pl.BlockSpec(memory_space=s) for _, s in ins] + [pl.BlockSpec(memory_space=ANY)] * late,
        out_specs=[pl.BlockSpec(memory_space=s) for _, _, s in outs],
        out_shape=[s(shape, dtype) for shape, dtype, s in outs],
        scratch_shapes=scratch,
        input_output_aliases=aliases or {},
        cost_estimate=pl.CostEstimate(flops=int(micros * pace), bytes_accessed=0, transcendentals=0),
        compiler_params=pltpu.CompilerParams(vmem_limit_bytes=vmem * 2**20),
    )(*[placed(a, s) for a, s in ins], *after)


def rows(ref, at, size):
    return ref.at[pl.ds(pl.multiple_of(at * size, size), size), :]


def pair_sums(size, own, other, places, code, keep):
    step = 64

    def summed(k, at):
        there = pl.ds(pl.multiple_of(places[k] * size + at, step), step)
        return own[k * size + at : k * size + at + step, :].astype(jnp.float32) + other[there, :].astype(jnp.float32)

    for at in range(0, size, step):
        code[at : at + step, :] = encode(summed(0, at), 2)
        keep[at : at + step, :] = summed(1, at)


def fetch_kernel(size, stale, grad, first_own, second_own, grad_out, sem):
    core, first, _ = place(lax.axis_index("worker"))
    copies = [
        pltpu.make_async_copy(
            rows(stale, block(core, half, sub), size), own.at[k * size : (k + 1) * size, :], sem.at[2 * sub + k]
        )
        for sub, own in enumerate((first_own, second_own))
        for k, half in enumerate((1 - first, first))
    ]
    copies.append(pltpu.make_async_copy(grad, grad_out, sem.at[4]))
    for copy in copies:
        copy.start()
    for copy in copies:
        copy.wait()


def pair_kernel(size, sub, own, other, code, keep):
    core, first, _ = place(lax.axis_index("worker"))
    places = [block(core, half, sub) for half in (1 - first, first)]
    pair_sums(size, own, other, places, code, keep)


def add_kernel(held, total, value, received, out, code):
    summed = value[...] + decode(received[...], held)
    out[...] = summed
    code[...] = encode(summed, total)


def keys_kernel(tokens, weights, grad, grad_far, packed, own, later, total):
    total[...] = jnp.dot(tokens[...], weights[...], preferred_element_type=jnp.float32)
    size = own.shape[0]
    shard = lax.axis_index("fsdp")
    packed[:size, :] = grad[...]
    packed[size : 2 * size, :] = grad_far[...]
    for k, d in enumerate((1, 3)):
        value = rows(total, shard ^ d, size)[...]
        high = value.astype(jnp.bfloat16)
        packed[(2 + k) * size : (3 + k) * size, :] = high
        packed[(4 + k) * size : (5 + k) * size, :] = (value - high.astype(jnp.float32)).astype(jnp.bfloat16)
    own[...] = rows(total, shard, size)[...]
    later[...] = rows(total, shard ^ 2, size)[...]


def keys_add_kernel(received, own, later, own_out, later_out):
    size = own.shape[0]

    def arrived(k):
        high, low = (received[at * size : (at + 1) * size, :].astype(jnp.float32) for at in (2 + k, 4 + k))
        return high + low

    own_out[...] = own[...] + arrived(0)
    later_out[...] = later[...] + arrived(1)


def relay_kernel(*refs):
    half = len(refs) // 2
    for source, target in zip(refs[:half], refs[half:], strict=True):
        target[...] = source[...]


def spots(me):
    core, first, last = place(me)
    return {
        "own": (core, first),
        "near": (core, 1 - first),
        "across": (1 - core, last),
        "far": (1 - core, 1 - last),
    }


def span_of(size, kind, sub):
    return pl.ds(pl.multiple_of(block(*spots(lax.axis_index("worker"))[kind], sub) * size, size), size)


def fresh_kernel(workers, soon, late, tokens, weights, anchor, momentum, stale, near, far, *rest):
    sums, rest = rest[: len(soon)], rest[len(soon) :]
    fresh_out, grad_out, param_out, moment_out, rest = *rest[:4], rest[4:]
    bases, rest = rest[: len(late)], rest[len(late) :]
    fresh_buf, grad_buf, param_buf, moment, portion, sem = rest
    size = weights.shape[0] // workers
    copies = []

    def send(source, target):
        copies.append(pltpu.make_async_copy(source, target, sem.at[len(copies)]))
        copies[-1].start()

    held = portion.shape[0] // 4
    shard = lax.axis_index("fsdp")
    for d, source, k in ((0, near, 0), (2, near, 1), (1, far, 0), (3, far, 1)):
        rows(portion, shard ^ d, held)[...] = source[k * held : (k + 1) * held, :]
    for k, which in enumerate([*soon, *late]):
        span = span_of(size, *which)
        weight = weights[span, :]
        grad_weight = lax.dot_general(
            tokens[:, span], portion[...], (((0,), (0,)), ((), ())), preferred_element_type=jnp.float32
        )
        grad_buf[k] = lax.dot_general(
            portion[...], weight, (((1,), (1,)), ((), ())), preferred_element_type=jnp.float32
        ).astype(jnp.bfloat16)
        send(grad_buf.at[k], grad_out.at[:, span])
        value = anchor[span, :]
        fresh = value - (weight.astype(jnp.float32) - inner_rate * grad_weight)
        fresh_buf[k] = fresh.astype(jnp.bfloat16)
        send(fresh_buf.at[k], fresh_out.at[span, :])
        base = value - outer_rate * (
            outer_momentum * outer_momentum * momentum[span, :]
            + (fresh - stale[span, :].astype(jnp.float32)) / workers
        )
        if k >= len(soon):
            bases[k - len(soon)][...] = base
        else:
            param_buf[k] = finished(which[0], workers, base, sums[k])
            send(param_buf.at[k], param_out.at[span, :])
        if k == 0:
            _, _, last = place(lax.axis_index("worker"))
            average = jnp.where(last == 0, sums[0][...], sums[1][...]) / workers
            moment[...] = outer_momentum * rows(momentum, lax.axis_index("worker"), size)[...] + average
            send(moment, moment_out)
    for copy in copies:
        copy.wait()


def finished(kind, workers, base, piece):
    total = piece[...]
    if kind != "own":
        total = decode(total, workers)
    return (base - (outer_rate * (1.0 + outer_momentum) / workers) * total).astype(jnp.bfloat16)


def update_kernel(workers, kinds, keys, *rest):
    count = len(kinds)
    bases, pieces, rest = rest[:count], rest[count : 2 * count], rest[2 * count :]
    if keys:
        own, received, _, out, key_out, out_buf, key_buf, sem = rest
    else:
        _, out, out_buf, sem = rest
    size = out.shape[0] // workers
    copies = []
    if keys:
        key_buf[...] = (own[...] + received[...]).astype(jnp.bfloat16)
        copies.append(pltpu.make_async_copy(key_buf, key_out, sem.at[2 * count]))
        copies[0].start()
    for k, which in enumerate(kinds):
        for part in range(2):
            some = pl.ds(part * (size // 2), size // 2)
            out_buf[k, some, :] = finished(which[0], workers, bases[k][some, :], pieces[k].at[some, :])
            there = pl.ds(pl.multiple_of(block(*spots(lax.axis_index("worker"))[which[0]], which[1]) * size + part * (size // 2), size // 2), size // 2)
            copies.append(pltpu.make_async_copy(out_buf.at[k, some, :], out.at[there, :], sem.at[2 * k + part]))
            copies[-1].start()
    for copy in copies:
        copy.wait()


def fast(tokens, inner_weight, key_grad, anchor, momentum, stale_delta):
    workers, shards = lax.axis_size("worker"), lax.axis_size("fsdp")
    f32, bf16 = jnp.float32, jnp.bfloat16
    DMA = pltpu.SemaphoreType.DMA
    weights, stale = inner_weight[0], stale_delta[0]
    height, columns = stale.shape
    batch = tokens.shape[0]
    size = height // workers
    window = (size, columns)

    def swap(value, flips):
        return lax.ppermute(value, "worker", [(i, i ^ flips[i % 2]) for i in range(workers)])

    def across_shards(value, distance):
        return lax.ppermute(value, "fsdp", [(i, i ^ distance) for i in range(shards)])

    beside, first, last = (1, 1), (2, 4), (4, 2)
    chunks = range(2)

    key_rows = batch // shards
    other = swap(stale, beside)
    block_of_keys = (key_rows, columns)
    *owns, grad = call(
        functools.partial(fetch_kernel, size),
        [(stale, HBM), (key_grad, HBM)],
        [((2 * size, columns), bf16, VMEM)] * 2 + [(key_grad.shape, bf16, VMEM)],
        scratch=[DMA((5,))],
        micros=cost["fetch"],
    )
    grad_far = across_shards(grad, 2)

    codes, keeps = [], []
    for c in chunks:
        code, keep = call(
            functools.partial(pair_kernel, size, c),
            [(owns[c], VMEM), (other, VMEM)],
            [(window, bf16, VMEM), (window, f32, VMEM)],
            after=keeps,
            micros=cost["pair"][c],
        )
        codes.append(code)
        keeps.append(keep)
    got = [swap(codes[c], first) for c in chunks]

    packed, own_keys, later_keys = call(
        keys_kernel,
        [(tokens, VMEM), (weights, VMEM), (grad, VMEM), (grad_far, VMEM)],
        [((6 * key_rows, columns), bf16, VMEM), (block_of_keys, f32, VMEM), (block_of_keys, f32, VMEM)],
        scratch=[pltpu.VMEM((batch, columns), f32)],
        after=[keeps[1]],
        micros=cost["keys"],
    )
    arrived = across_shards(packed, 1)
    grads = [packed, arrived]

    def added(held, total, before_second):
        for c in chunks:
            keeps[c], codes[c] = call(
                functools.partial(add_kernel, held, total),
                [(keeps[c], VMEM), (got[c], VMEM)],
                [(window, f32, VMEM), (window, bf16, VMEM)],
                after=[] if c == 0 else [keeps[0], *before_second],
                micros=cost["add"][c],
            )

    late_kinds = [("near", 0), ("far", 0), ("near", 1), ("far", 1)]
    added(2, 4, [packed])
    got = [swap(codes[c], last) for c in chunks]
    own_keys, later_keys = call(
        keys_add_kernel,
        [(arrived, VMEM), (own_keys, VMEM), (later_keys, VMEM)],
        [(block_of_keys, f32, VMEM), (block_of_keys, f32, VMEM)],
        after=[keeps[1]],
        micros=cost["keys_add"],
    )
    key_far = across_shards(later_keys, 2)
    added(4, 8, [own_keys])
    near = [swap(codes[c], first) for c in chunks]
    across = [swap(codes[c], beside) for c in chunks]
    soon_kinds = [("own", 0), ("own", 1), ("across", 0), ("across", 1)]
    late_kinds = [("near", 0), ("near", 1), ("far", 0), ("far", 1)]
    n = len(soon_kinds)
    ins = [tokens, weights, anchor, momentum, stale, packed, arrived, *keeps, *across]
    fresh_out, grad_input, updated, new_moment, *bases = call(
        functools.partial(fresh_kernel, workers, soon_kinds, late_kinds),
        [(value, VMEM) for value in ins],
        [
            ((height, columns), bf16, HBM),
            ((batch, height), bf16, HBM),
            ((height, columns), bf16, HBM),
            (window, f32, HBM),
        ]
        + [(window, f32, VMEM)] * n,
        scratch=[
            pltpu.VMEM((2 * n, *window), bf16),
            pltpu.VMEM((2 * n, batch, size), bf16),
            pltpu.VMEM((n, *window), bf16),
            pltpu.VMEM(window, f32),
            pltpu.VMEM((batch, columns), bf16),
            DMA((5 * n + 1,)),
        ],
        micros=cost["fresh"],
    )
    relayed = call(
        relay_kernel, [(v, VMEM) for v in near], [(window, bf16, VMEM)] * 2, after=[bases[0]], micros=cost["relay"]
    )
    far = [swap(v, beside) for v in relayed]

    pieces = [*near, *far]
    for which, with_keys in (((0, 1), False), ((2, 3), True)):
        ins = [(bases[w], VMEM) for w in which] + [(pieces[w], VMEM) for w in which]
        outs = [((height, columns), bf16, HBM)]
        scratch = [pltpu.VMEM((len(which), *window), bf16)]
        if with_keys:
            ins += [(own_keys, VMEM), (key_far, VMEM)]
            outs.append(((key_rows, columns), bf16, HBM))
            scratch.append(pltpu.VMEM((key_rows, columns), bf16))
        ins.append((updated, HBM))
        updated, *key_out = call(
            functools.partial(update_kernel, workers, [late_kinds[w] for w in which], with_keys),
            ins,
            outs,
            scratch=[*scratch, DMA((2 * len(which) + 1,))],
            aliases={len(ins) - 1: 0},
            micros=cost["update"][with_keys],
        )
    return key_out[0], grad_input, updated[None], new_moment, fresh_out[None]


def plain(tokens, inner_weight, key_grad, anchor, momentum, stale_delta):
    weights = inner_weight[0]
    key_out = lax.psum_scatter(
        jnp.dot(tokens, weights, preferred_element_type=jnp.float32), "fsdp", scatter_dimension=0, tiled=True
    ).astype(jnp.bfloat16)
    portion = lax.all_gather(key_grad, "fsdp", axis=0, tiled=True)
    grad_weight = lax.dot_general(tokens, portion, (((0,), (0,)), ((), ())), preferred_element_type=jnp.float32)
    grad_input = lax.dot_general(portion, weights, (((1,), (1,)), ((), ())), preferred_element_type=jnp.float32)
    fresh_term = anchor - (weights.astype(jnp.float32) - inner_rate * grad_weight)
    stale_value = stale_delta[0].astype(jnp.float32)
    workers = lax.axis_size("worker")
    average = lax.psum(stale_value, "worker") / workers
    moment_full = outer_momentum * momentum + average
    common_term = average + outer_momentum * moment_full
    share_rows = anchor.shape[0] // workers
    new_moment = lax.dynamic_slice_in_dim(moment_full, lax.axis_index("worker") * share_rows, share_rows, 0)
    updated = anchor - outer_rate * (common_term + (fresh_term - stale_value) / workers)
    return (
        key_out,
        grad_input.astype(jnp.bfloat16),
        updated[None].astype(jnp.bfloat16),
        new_moment,
        fresh_term[None].astype(jnp.bfloat16),
    )


def local(*args):
    tokens, inner_weight = args[:2]
    workers, shards = lax.axis_size("worker"), lax.axis_size("fsdp")
    size = inner_weight.shape[1] // workers
    fits = workers == 2**3 and shards == 2**2
    fits = fits and size % 128 == 0 and tokens.shape[0] // shards % 16 == 0
    return (fast if fits else plain)(*args)


def solution(mesh):
    in_specs = (
        P("worker", "fsdp"),
        P("worker", "fsdp", None),
        P(("worker", "fsdp"), None),
        P("fsdp", None),
        P("fsdp", None),
        P("worker", "fsdp", None),
    )
    out_specs = (
        P(("worker", "fsdp"), None),
        P("worker", "fsdp"),
        P("worker", "fsdp", None),
        P(("fsdp", "worker"), None),
        P("worker", "fsdp", None),
    )
    return jax.shard_map(local, mesh=mesh, in_specs=in_specs, out_specs=out_specs, check_vma=False)
```
